32 devices in a mesh: dp: 8 (over z, y), blk: 4 (over x, core).
Axes of the slice: x: 2, y: 2, z: 4, core: 2. Of those that a mesh axis runs over, the one named last changes fastest.
Arguments:
- embedded: bfloat16 [16, 2048, 768], P('dp', 'blk'), may hold values from -6 to 6
- species_flag: int32 [16], P('dp'), may hold values 0 or 1
- gene_ids: int32 [16, 2048], P('dp', 'blk'), may hold values from 0 to 35999, as said below
- species_table: float32 [2, 768], replicated, may hold values from -3 to 3
- norm_gain: float32 [2, 2, 768], replicated, may hold values from 0.1 to 1.9
- norm_bias: float32 [2, 2, 768], replicated, may hold values from -1.8 to 1.8
- w_qkv: bfloat16 [2, 768, 2304], replicated, may hold values from -0.3125 to 0.3125
- w_out: bfloat16 [2, 768, 768], replicated, may hold values from -0.875 to 0.875
- w_up: bfloat16 [2, 768, 3072], replicated, may hold values from -0.21875 to 0.21875
- w_down: bfloat16 [2, 3072, 768], replicated, may hold values from -0.109375 to 0.109375
- out_cotangent: bfloat16 [16, 2048, 768], P('dp', 'blk'), may hold values from -6 to 6
Outputs:
- hidden_out: float32 [16, 2048, 768], P('dp', 'blk')
- embed_grad: float32 [16, 2048, 768], P('dp', 'blk')
- species_grad: float32 [2, 768], replicated
- gain_grad: float32 [2, 2, 768], replicated
- bias_grad: float32 [2, 2, 768], replicated
- w_qkv_grad: float32 [2, 768, 2304], P(None, 'dp', 'blk')
- w_out_grad: float32 [2, 768, 768], P(None, 'dp', 'blk')
- w_up_grad: float32 [2, 768, 3072], P(None, 'dp', 'blk')
- w_down_grad: float32 [2, 3072, 768], P(None, 'dp', 'blk')
The draws below stay inside these ranges and needn't reach their ends.
Inputs may be any that keep to these rules, and one draw needn't show every extreme that they name: `gene_ids`: in each cell the nonzero ids form a leading run of one or more positions and all later positions are 0 (padding); in each group of 2 consecutive cells one cell has no padding.
All inputs are finite; a program needn't handle non-finite values. No bound on the sum of `species_flag` on one device may be relied on, other than what follows from the above.
Results may differ from the reference program's by a relative error of at most 0.017.
Values may be sent and summed in bfloat16 or wider, within the bound.
No kernel may reach another device: no remote copies, remote signals or barrier semaphores. Data moves between devices by JAX's collectives and lax.ppermute only.
A program may use at most 704 MiB of HBM per device.

```python
import math
import jax
import jax.numpy as jnp
from jax import lax

D = 768
HEADS = 12
HEAD_DIM = 64
FF = 3072
GENES = 2048
LAYERS = 2
VOCAB = 36000
CELLS_GRP = 2
CELLS = 16


def draw_gene_ids(key, part):
    key = jax.random.fold_in(key, 11)
    key_len, key_pick, key_ids = jax.random.split(key, 3)
    lengths = jax.random.randint(key_len, (CELLS,), GENES // 8, GENES // 2 + 1)
    chosen = jax.random.randint(key_pick, (CELLS // CELLS_GRP,), 0, CELLS_GRP)
    within = jnp.arange(CELLS, dtype=jnp.int32) % CELLS_GRP
    full_cell = within == jnp.repeat(chosen, CELLS_GRP)
    lengths = jnp.where(full_cell, GENES, lengths)
    identity = jax.random.randint(key_ids, (CELLS, GENES), 1, VOCAB)
    position = jnp.arange(GENES, dtype=jnp.int32)
    return jnp.where(position[None, :] < lengths[:, None], identity, 0).astype(jnp.int32)


def set_ends(entries, rng, least, largest):
    extent = entries.shape
    index_at = [jax.random.randint(jax.random.fold_in(rng, axis), (), 0, extent[axis]) for axis in range(len(extent))]
    entries = entries.at[tuple(index_at)].set(least)
    longest = extent.index(max(extent))
    index_at[longest] = (index_at[longest] + 1) % extent[longest]
    return entries.at[tuple(index_at)].set(largest)


def block_scale(own_key, extent, cuts, low, high):
    def one(dim, parts):
        draws = jax.random.uniform(jax.random.fold_in(jax.random.fold_in(own_key, 6), dim), (parts,), jnp.float32, low / len(cuts), high / len(cuts))
        return jnp.repeat(jnp.exp(draws), extent[dim] // parts).reshape((-1,) + (1,) * (len(extent) - dim - 1))

    level = one(*cuts[0])
    for cut in cuts[1:]:
        level = level * one(*cut)
    return level


def gaussian(own_key, extent, width, bound, shards=(), kind=jnp.bfloat16):
    values = jax.random.normal(own_key, extent, jnp.float32) * width
    if len(shards) > 0:
        values = block_scale(own_key, extent, shards, -0.22, 0.18) * values
    return jnp.clip(values, min=-bound, max=bound).astype(kind)


def setup_inputs(seed: int = 0) -> dict:
    key_list = jax.random.split(jax.random.key(seed), 12)
    return {
        "embedded": gaussian(key_list[0], (CELLS, GENES, D), 1.0, 6.0, ((0, 8), (1, 4))),
        "species_flag": set_ends((jax.random.randint(key_list[1], (CELLS,), 0, 3) < 1).astype(jnp.int32), jax.random.fold_in(key_list[1], 1), 0, 1),
        "gene_ids": draw_gene_ids(jax.random.fold_in(key_list[11], 71), 0),
        "species_table": gaussian(key_list[3], (2, D), 0.5, 3.0, (), jnp.float32),
        "norm_gain": jnp.clip(1.0 + 0.18 * jax.random.normal(key_list[4], (LAYERS, 2, D), jnp.float32), 0.1, 1.9),
        "norm_bias": gaussian(key_list[5], (LAYERS, 2, D), 0.3, 1.8, (), jnp.float32),
        "w_qkv": gaussian(key_list[6], (LAYERS, D, 3 * D), (D // 2) ** -0.5, 0.3125),
        "w_out": gaussian(key_list[7], (LAYERS, D, D), (D // 16) ** -0.5, 0.875),
        "w_up": gaussian(key_list[8], (LAYERS, D, FF), D ** -0.5, 0.21875),
        "w_down": gaussian(key_list[9], (LAYERS, FF, D), FF ** -0.5, 0.109375),
        "out_cotangent": gaussian(key_list[10], (CELLS, GENES, D), 1.0, 6.0, ((0, 8), (1, 4))),
    }


@jax.custom_vjp
def low(v):
    return lax.optimization_barrier(v.astype(jnp.bfloat16)).astype(jnp.float32)

@jax.custom_vjp
def low_back(v):
    return v

def low_keep(v):
    return (low(v), None)

def low_pass(kept, grad):
    return (grad,)

def back_keep(v):
    return (v, None)

def back_low(kept, grad):
    return (low(grad),)
low.defvjp(low_keep, low_pass)
low_back.defvjp(back_keep, back_low)

def exact_dot(left, right):
    return jnp.dot(left, right, precision=lax.Precision.HIGHEST, preferred_element_type=jnp.float32)

def layer_norm(value, gain, bias):
    mean = lax.optimization_barrier(jnp.mean(value, axis=-1, keepdims=True))
    centred = value - mean
    variance = lax.optimization_barrier(jnp.mean(centred * centred, axis=-1, keepdims=True))
    return centred * lax.rsqrt(variance + 1e-05) * gain + bias

def cell_forward(params, state, valid):
    gain, bias, wqkv, wout, wup, wdown = params
    scale = 1.0 / math.sqrt(HEAD_DIM)
    for layer in range(LAYERS):
        normed = low(layer_norm(state, gain[layer, 0], bias[layer, 0]))
        qkv = low(low_back(exact_dot(normed, wqkv[layer])))
        queries = qkv[:, :D].reshape(GENES, HEADS, HEAD_DIM)
        keys = qkv[:, D:2 * D].reshape(GENES, HEADS, HEAD_DIM)
        values = qkv[:, 2 * D:].reshape(GENES, HEADS, HEAD_DIM)
        scores = jnp.einsum('qhd,khd->hqk', queries, keys, precision=lax.Precision.HIGHEST) * scale
        scores = low_back(scores)
        scores = jnp.where(valid[None, None, :], scores, -1e+30)
        shifted = jnp.exp(scores - lax.optimization_barrier(jnp.max(scores, axis=-1, keepdims=True)))
        probs = low(shifted / lax.optimization_barrier(jnp.sum(shifted, axis=-1, keepdims=True)))
        attended = jnp.einsum('hqk,khd->qhd', probs, values, precision=lax.Precision.HIGHEST)
        attended = low(low_back(attended.reshape(GENES, D)))
        state = state + low_back(exact_dot(attended, wout[layer]))
        normed_two = low(layer_norm(state, gain[layer, 1], bias[layer, 1]))
        upward = low_back(exact_dot(normed_two, wup[layer]))
        active = low(jax.nn.gelu(upward, approximate=False))
        state = state + low_back(exact_dot(active, wdown[layer]))
    return state

def reference(embedded, species_flag, gene_ids, species_table, norm_gain, norm_bias, w_qkv, w_out, w_up, w_down, out_cotangent):
    valid = gene_ids != 0

    def forward(emb, table, gain, bias, wqkv, wout, wup, wdown):
        start = emb + table[species_flag][:, None, :]
        params = (gain, bias, wqkv, wout, wup, wdown)

        def one_cell(pair):
            return cell_forward(params, pair[0], pair[1])
        return lax.map(jax.checkpoint(one_cell), (start, valid))
    hidden_out, pullback = jax.vjp(forward, embedded.astype(jnp.float32), species_table, norm_gain, norm_bias, w_qkv.astype(jnp.float32), w_out.astype(jnp.float32), w_up.astype(jnp.float32), w_down.astype(jnp.float32))
    grads = pullback(out_cotangent.astype(jnp.float32))
    return (hidden_out, grads[0], grads[1], grads[2], grads[3], grads[4], grads[5], grads[6], grads[7])
```

```python
import functools
import math

import jax
import jax.numpy as jnp
from jax import lax
from jax.experimental import pallas as pl
from jax.experimental.pallas import tpu as pltpu
from jax.sharding import PartitionSpec as P

HEADS = 12
HEAD_DIM = 64
LAYERS = 2
PAIR = 2 * HEAD_DIM
EPS = 1e-05
LOG2E = 1.4426950408889634
LN2 = 0.6931471805599453
SCALE = 1.0 / math.sqrt(HEAD_DIM)
MASKED = -1e30
MIB = 1024 * 1024

F32 = jnp.float32
BF16 = jnp.bfloat16


def mm(left, right):
    return jnp.dot(left, right, preferred_element_type=F32)


def mm_nt(left, right):
    return lax.dot_general(left, right, (((1,), (1,)), ((), ())), preferred_element_type=F32)


def mm_tn(left, right):
    return lax.dot_general(left, right, (((0,), (0,)), ((), ())), preferred_element_type=F32)


def pieced(product, left, right, axis):
    wide = right.shape[axis]
    pieces = [
        product(
            left[...],
            right[:, at : min(at + 256, wide)]
            if axis == 1
            else right[at : min(at + 256, wide), :],
        )
        for at in range(0, wide, 256)
    ]
    return pieces[0] if len(pieces) == 1 else jnp.concatenate(pieces, axis=1)


def normalise(value):
    mean = jnp.mean(value, axis=-1, keepdims=True)
    centred = value - mean
    variance = jnp.mean(centred * centred, axis=-1, keepdims=True)
    r = lax.rsqrt(variance + EPS)
    return centred * r, r


def norm_backward(n, r, e, gain):
    eg = e * gain
    first = jnp.mean(eg, axis=-1, keepdims=True)
    second = jnp.mean(eg * n, axis=-1, keepdims=True)
    return r * (eg - first - n * second)


def params(mib=64):
    return pltpu.CompilerParams(vmem_limit_bytes=mib * MIB)


def whole(shape):
    return pl.BlockSpec(shape, lambda i: (0,) * len(shape), pipeline_mode=pl.Buffered(1))


def rows_of(tile, width):
    return pl.BlockSpec((tile, width), lambda i: (i, 0))


def slabs_of(count, tile, width):
    return pl.BlockSpec((count, tile, width), lambda i: (0, i, 0))


def columns_of(width, tile):
    return pl.BlockSpec((width, tile), lambda i: (0, i))


def layer_of(stacked, layer):
    rest = stacked.shape[1:]
    return pl.BlockSpec(
        (None,) + rest, lambda i: (layer,) + (0,) * len(rest), pipeline_mode=pl.Buffered(1)
    )


def ordered(after):
    return [pl.BlockSpec(memory_space=pl.ANY)] * len(after)


def without(kernel, first, count):
    def run(*refs):
        return kernel(*refs[:first], *refs[first + count :])

    return run


def turned(value):
    return value.T.astype(BF16)


class Tokens:
    def __init__(self, arrays, shift=None):
        self.arrays = arrays
        self.shift = shift
        self.rows = sum(array.shape[0] for array in arrays)
        self.width = arrays[0].shape[1]

    def operands(self):
        return list(self.arrays) + ([] if self.shift is None else [self.shift])

    def specs(self, tile):
        tiles = self.arrays[0].shape[0] // tile
        if len(self.arrays) == 1:
            specs = [rows_of(tile, self.width)]
        else:
            specs = [
                pl.BlockSpec((tile, self.width), lambda i: (jnp.minimum(i, tiles - 1), 0)),
                pl.BlockSpec((tile, self.width), lambda i: (jnp.maximum(i - tiles, 0), 0)),
            ]
        return specs + ([] if self.shift is None else [whole((1, self.width))])

    def count(self):
        return len(self.operands())

    def read(self, tile, refs):
        value = refs[0][...].astype(F32)
        if tile == self.rows and len(self.arrays) == 2:
            value = jnp.concatenate([value, refs[1][...].astype(F32)], axis=0)
        elif len(self.arrays) == 2:
            first = pl.program_id(0) < self.arrays[0].shape[0] // tile
            value = jnp.where(first, value, refs[1][...].astype(F32))
        return value if self.shift is None else value + refs[-1][...]


def qkv_kernel(x, tile, *refs):
    gain_ref, bias_ref, w_ref, h_ref, q_ref, kv_ref = refs[x.count() :]
    width = x.width
    n, _ = normalise(x.read(tile, refs[: x.count()]))
    h = n * gain_ref[0:1, :] + bias_ref[0:1, :]
    h_ref[...] = turned(h)
    h = h.astype(BF16)
    kv_ref[...] = mm(h, w_ref[:, width:]).astype(BF16)
    q_ref[...] = (mm(h, w_ref[:, :width]) * (SCALE * LOG2E)).astype(BF16)


def qkv_forward(layer, x, gain, bias, w, after):
    rows, width = x.rows, x.width
    tile = min(256, rows // 2)
    return pl.pallas_call(
        without(functools.partial(qkv_kernel, x, tile), x.count() + 3, len(after)),
        grid=(rows // tile,),
        in_specs=x.specs(tile)
        + [layer_of(value, layer) for value in (gain, bias, w)]
        + ordered(after),
        out_specs=[columns_of(width, tile), rows_of(tile, width), rows_of(tile, 2 * width)],
        out_shape=[
            jax.ShapeDtypeStruct((width, rows), BF16),
            jax.ShapeDtypeStruct((rows, width), BF16),
            jax.ShapeDtypeStruct((rows, 2 * width), BF16),
        ],
        compiler_params=params(),
        cost_estimate=pl.CostEstimate(
            flops=6 * rows * width * width, bytes_accessed=12 * rows * width, transcendentals=0
        ),
        name="norm_qkv",
    )(*x.operands(), gain, bias, w, *after)


def lanes_like(shape):
    lane = lax.broadcasted_iota(jnp.int32, shape, 1)
    return lane < HEAD_DIM, lane & (HEAD_DIM - 1)


def three_parts(value, sub, fourth):
    high = value.astype(BF16).astype(F32)
    rest = value - high
    middle = rest.astype(BF16).astype(F32)
    least = rest - middle
    return jnp.where(
        sub == 0,
        high,
        jnp.where(sub == 1, middle, jnp.where(sub == 2, least, jnp.where(sub == 3, fourth, 0.0))),
    )


def attend_kernel(parts, *refs):
    q_ref = refs[0]
    k_refs = refs[1 : 1 + parts]
    v_refs = refs[1 + parts : 1 + 2 * parts]
    dead_refs = refs[1 + 2 * parts : 1 + 3 * parts]
    o_ref, inverse_ref, p_ref, ka, kb, va, vb = refs[1 + 3 * parts :]
    rows = k_refs[0].shape[0]

    @pl.when(pl.program_id(1) == 0)
    def _():
        low, sub = lanes_like((rows, PAIR))
        for part in range(parts):
            own = slice(part * rows, (part + 1) * rows)
            k = k_refs[part][...].astype(F32)
            v = v_refs[part][...].astype(F32)
            extra = jnp.where(sub == 3, dead_refs[part][...].astype(F32), 0.0)
            ka[own, :] = jnp.where(low, k, extra).astype(BF16)
            kb[own, :] = jnp.where(low, extra, k).astype(BF16)
            va[own, :] = jnp.where(low, v, 1.0).astype(BF16)
            vb[own, :] = jnp.where(low, 1.0, v).astype(BF16)

    low, sub = lanes_like(q_ref.shape)
    fourth = jnp.where(sub == 3, 1.0, 0.0)
    q = q_ref[...].astype(F32)
    sa = mm_nt(jnp.where(low, q, fourth).astype(BF16), ka[...])
    sb = mm_nt(jnp.where(low, fourth, q).astype(BF16), kb[...])
    pa = jnp.exp2(sa - jnp.max(sa, axis=-1, keepdims=True)).astype(BF16)
    p_ref[0] = pa
    oa = mm(pa, va[...])
    pb = jnp.exp2(sb - jnp.max(sb, axis=-1, keepdims=True)).astype(BF16)
    p_ref[1] = pb
    ob = mm(pb, vb[...])
    inverse = 1.0 / pltpu.roll(jnp.where(low, ob, oa), HEAD_DIM, 1)
    inverse_ref[...] = inverse
    o_ref[...] = (jnp.where(low, oa, ob) * inverse).astype(BF16)


def attend(q, kv_parts, dead_parts):
    rows, width = q.shape
    parts = len(kv_parts)
    pairs = width // PAIR
    tile = min(512, rows)
    keys = parts * rows
    some = pl.BlockSpec((tile, PAIR), lambda j, i: (i, j))
    first = pl.BlockSpec((rows, PAIR), lambda j, i: (0, j))
    second = pl.BlockSpec((rows, PAIR), lambda j, i: (0, pairs + j))
    fixed = pl.BlockSpec((rows, PAIR), lambda j, i: (0, 0))
    scratch = pltpu.VMEM((keys, PAIR), BF16)
    return pl.pallas_call(
        functools.partial(attend_kernel, parts),
        grid=(pairs, rows // tile),
        in_specs=[some] + [first] * parts + [second] * parts + [fixed] * parts,
        out_specs=[some, some, pl.BlockSpec((2, tile, keys), lambda j, i: (j, i, 0))],
        out_shape=[
            jax.ShapeDtypeStruct((rows, width), BF16),
            jax.ShapeDtypeStruct((rows, width), F32),
            jax.ShapeDtypeStruct((2 * pairs, rows, keys), BF16),
        ],
        scratch_shapes=[scratch] * 4,
        compiler_params=params(),
        cost_estimate=pl.CostEstimate(
            flops=16 * rows * keys * width,
            bytes_accessed=4 * pairs * rows * keys,
            transcendentals=HEADS * rows * keys,
        ),
        name="attend",
    )(q, *kv_parts, *kv_parts, *dead_parts)


def attend_back_kernel(parts, *refs):
    q_ref, inverse_ref, att_ref, datt_ref, p_ref = refs[:5]
    k_refs = refs[5 : 5 + parts]
    v_refs = refs[5 + parts : 5 + 2 * parts]
    rest = refs[5 + 2 * parts :]
    dq_ref = rest[0]
    dkv_refs = rest[1 : 1 + parts]
    ks, va, vb, dk_turned, dv_turned = rest[1 + parts :]
    rows = k_refs[0].shape[0]
    index = pl.program_id(1)

    @pl.when(index == 0)
    def _():
        low, sub = lanes_like((rows, PAIR))
        ones = jnp.where(sub < 3, 1.0, 0.0)
        for part in range(parts):
            own = slice(part * rows, (part + 1) * rows)
            ks[own, :] = k_refs[part][...]
            v = v_refs[part][...].astype(F32)
            va[own, :] = jnp.where(low, v, ones).astype(BF16)
            vb[own, :] = jnp.where(low, ones, v).astype(BF16)
        dk_turned[...] = jnp.zeros_like(dk_turned)
        dv_turned[...] = jnp.zeros_like(dv_turned)

    low, sub = lanes_like(q_ref.shape)
    q_turned = turned(q_ref[...].astype(F32))
    datt = datt_ref[...].astype(F32) * inverse_ref[...]
    datt_turned = turned(datt)
    product = datt * att_ref[...].astype(F32)
    term_a = jnp.sum(jnp.where(low, product, 0.0), axis=-1, keepdims=True)
    term_b = jnp.sum(jnp.where(low, 0.0, product), axis=-1, keepdims=True)
    extra = three_parts(-jnp.where(low, term_b, term_a), sub, 0.0)
    ta = mm_nt(jnp.where(low, datt, extra).astype(BF16), va[...])
    tb = mm_nt(jnp.where(low, extra, datt).astype(BF16), vb[...])
    first, second = slice(0, HEAD_DIM), slice(HEAD_DIM, PAIR)
    pa, pb = p_ref[0], p_ref[1]
    dv_turned[first, :] += mm(datt_turned[first, :], pa)
    ga = (pa.astype(F32) * ta).astype(BF16)
    dqa = mm(ga, ks[...])
    dk_turned[first, :] += mm(q_turned[first, :], ga)
    dv_turned[second, :] += mm(datt_turned[second, :], pb)
    gb = (pb.astype(F32) * tb).astype(BF16)
    dqb = mm(gb, ks[...])
    dk_turned[second, :] += mm(q_turned[second, :], gb)
    dq_ref[...] = (jnp.where(low, dqa, dqb) * SCALE).astype(BF16)

    @pl.when(index == pl.num_programs(1) - 1)
    def _():
        for part in range(parts):
            own = slice(part * rows, (part + 1) * rows)
            dkv_refs[part][0] = (dk_turned[:, own].T * LN2).astype(BF16)
            dkv_refs[part][1] = dv_turned[:, own].T.astype(BF16)


def attend_back(group, groups, q, inverse, att, datt, p, kv_parts, after):
    rows, width = q.shape
    parts = len(kv_parts)
    pairs = width // PAIR
    count = pairs // groups
    base = group * count
    tile = min(512, rows)
    keys = parts * rows
    some = pl.BlockSpec((tile, PAIR), lambda j, i: (i, base + j))
    first = pl.BlockSpec((rows, PAIR), lambda j, i: (0, base + j))
    second = pl.BlockSpec((rows, PAIR), lambda j, i: (0, pairs + base + j))
    both = pl.BlockSpec((2, rows, PAIR), lambda j, i: (0, 0, j))
    all_keys = pltpu.VMEM((keys, PAIR), BF16)
    turned_keys = pltpu.VMEM((PAIR, keys), F32)
    out = pl.pallas_call(
        without(functools.partial(attend_back_kernel, parts), 5 + 2 * parts, len(after)),
        grid=(count, rows // tile),
        in_specs=[some] * 4
        + [pl.BlockSpec((2, tile, keys), lambda j, i: (base + j, i, 0))]
        + [first] * parts
        + [second] * parts
        + ordered(after),
        out_specs=[pl.BlockSpec((tile, PAIR), lambda j, i: (i, j))] + [both] * parts,
        out_shape=[jax.ShapeDtypeStruct((rows, count * PAIR), BF16)]
        + [jax.ShapeDtypeStruct((2, rows, count * PAIR), BF16)] * parts,
        scratch_shapes=[all_keys] * 3 + [turned_keys] * 2,
        compiler_params=params(),
        cost_estimate=pl.CostEstimate(
            flops=32 * rows * keys * width // groups,
            bytes_accessed=4 * count * rows * keys,
            transcendentals=0,
        ),
        name="attend_back",
    )(q, inverse, att, datt, p, *kv_parts, *kv_parts, *after)
    return out[0], out[1:]


def gelu_parts(u):
    base = 1.0 + (0.3275911 * math.sqrt(0.5)) * jnp.abs(u)
    t = pl.reciprocal(base, approx=True)
    t = t * (2.0 - base * t)
    bell = jnp.exp2(u * u * (-0.5 * LOG2E))
    series = t * (
        0.5 * 0.254829592
        + t
        * (
            0.5 * -0.284496736
            + t * (0.5 * 1.421413741 + t * (0.5 * -1.453152027 + t * (0.5 * 1.061405429)))
        )
    )
    tail = series * bell
    share = jnp.where(u < 0.0, tail, 1.0 - tail)
    return u * share, share + u * bell * (1.0 / math.sqrt(2.0 * math.pi))


def pieces_of(rows, most):
    piece = min(most, rows)
    return [slice(at, at + piece) for at in range(0, rows, piece)]


def feed_kernel(x, tile, *refs):
    att_ref, wout_ref, gain_ref, bias_ref, wup_ref, wdown_ref = refs[x.count() : x.count() + 6]
    mid_ref, h_ref, att_turned_ref, act_ref, slope_ref, next_ref, h_kept = refs[x.count() + 6 :]

    @pl.when(pl.program_id(1) == 0)
    def _():
        middle = x.read(tile, refs[: x.count()]) + mm(att_ref[...], wout_ref[...])
        mid_ref[...] = middle
        next_ref[...] = middle
        att_turned_ref[...] = turned(att_ref[...].astype(F32))
        n, _ = normalise(middle)
        h = n * gain_ref[1:2, :] + bias_ref[1:2, :]
        h_ref[...] = turned(h)
        h_kept[...] = h.astype(BF16)

    pieces = pieces_of(tile, 512)
    ups = [mm(h_kept[pieces[0], :], wup_ref[...])]
    for i, piece in enumerate(pieces):
        if i + 1 < len(pieces):
            ups.append(mm(h_kept[pieces[i + 1], :], wup_ref[...]))
        active, slope = gelu_parts(ups[i])
        active = active.astype(BF16)
        act_ref[piece, :] = active
        slope_ref[piece, :] = slope.astype(BF16)
        next_ref[piece, :] += mm(active, wdown_ref[...])


def across(spec):
    return pl.BlockSpec(
        spec.block_shape, lambda i, c: spec.index_map(i), pipeline_mode=spec.pipeline_mode
    )


def feed_weights(layer, width, chunk):
    up = pl.BlockSpec((None, width, chunk), lambda i, c: (layer, 0, c))
    down = pl.BlockSpec((None, chunk, width), lambda i, c: (layer, c, 0))
    return up, down


def feed_forward(layer, att, x, wout, gain, bias, wup, wdown):
    rows, width = x.rows, x.width
    hidden = wup.shape[2]
    tile = min(512, rows // 2)
    chunk = 512
    wide = pl.BlockSpec((tile, chunk), lambda i, c: (i, c))
    return pl.pallas_call(
        functools.partial(feed_kernel, x, tile),
        grid=(rows // tile, hidden // chunk),
        in_specs=[
            across(spec)
            for spec in x.specs(tile)
            + [rows_of(tile, width)]
            + [layer_of(value, layer) for value in (wout, gain, bias)]
        ]
        + list(feed_weights(layer, width, chunk)),
        out_specs=[
            across(rows_of(tile, width)),
            across(columns_of(width, tile)),
            across(columns_of(width, tile)),
            wide,
            wide,
            across(rows_of(tile, width)),
        ],
        out_shape=[
            jax.ShapeDtypeStruct((rows, width), F32),
            jax.ShapeDtypeStruct((width, rows), BF16),
            jax.ShapeDtypeStruct((width, rows), BF16),
            jax.ShapeDtypeStruct((rows, hidden), BF16),
            jax.ShapeDtypeStruct((rows, hidden), BF16),
            jax.ShapeDtypeStruct((rows, width), F32),
        ],
        scratch_shapes=[pltpu.VMEM((tile, width), BF16)],
        compiler_params=params(),
        cost_estimate=pl.CostEstimate(
            flops=2 * rows * width * (width + 2 * hidden),
            bytes_accessed=16 * rows * width + 4 * rows * hidden + 4 * width * hidden,
            transcendentals=2 * rows * hidden,
        ),
        name="feed",
    )(*x.operands(), att, wout, gain, bias, wup, wdown)


def add_norm_sums(first_row, sum_ref, e, n):
    bias_row = first_row + 2 * LAYERS
    sum_ref[first_row : first_row + 1, :] += jnp.sum(e * n, axis=0, keepdims=True)
    sum_ref[bias_row : bias_row + 1, :] += jnp.sum(e, axis=0, keepdims=True)


def feed_back_kernel(layer, grad, dp_size, core_ref, *refs):
    count = grad.count()
    (
        slope_ref,
        act_ref,
        mid_ref,
        h_ref,
        att_ref,
        gain_ref,
        wup_ref,
        wdown_ref,
        wout_ref,
        start_ref,
        up_gone,
        up_kept,
        down_gone,
        down_kept,
        dmid_ref,
        datt_ref,
        sum_ref,
        gy_ref,
        gy_turned_ref,
        total_ref,
    ) = refs[count:]
    core = core_ref[0]
    step = pl.program_id(0)
    rows, width = gy_ref.shape
    chunk = slope_ref.shape[1]
    half = up_gone.shape[1]
    slabs = 2 * half
    deep = width // dp_size
    thin = width // slabs
    wide = up_gone.shape[3] - thin

    @pl.when(step == 0)
    def _():
        value = grad.read(rows, refs[:count])
        gy_ref[...] = value.astype(BF16)
        gy_turned = turned(value)
        for s in range(slabs):
            at = s // 2 * thin
            gy_turned_ref[s % 2, at : at + thin, :] = gy_turned[s * thin : (s + 1) * thin, :]
        total_ref[...] = jnp.zeros_like(total_ref)

    pieces = pieces_of(rows, 512)
    dups = []
    for piece in pieces:
        inner = mm_nt(gy_ref[piece, :], wdown_ref[...])
        dups.append((inner * slope_ref[piece, :].astype(F32)).astype(BF16))
    dup = dups[0] if len(dups) == 1 else jnp.concatenate(dups, axis=0)
    for piece, one in zip(pieces, dups):
        total_ref[piece, :] += mm_nt(one, wup_ref[...])
    for k in range(chunk // wide):
        slab = step * (chunk // wide) + k
        product = mm(h_ref[...], dup[:, k * wide : (k + 1) * wide]).astype(BF16)
        for goes, out_ref in ((slab % 2 != core, up_gone), (slab % 2 == core, up_kept)):

            @pl.when(goes)
            def _(product=product, out_ref=out_ref, slab=slab):
                for d in range(dp_size):
                    out_ref[d, slab // 2, :, :wide] = product[d * deep : (d + 1) * deep, :]

    active = act_ref[...]
    pair, _, _, across_wide = down_gone.shape
    for which, out_ref in ((1 - core, down_gone), (core, down_kept)):
        product = mm(gy_turned_ref[which], active).astype(BF16)
        for x in range(half):
            for d in range(pair):
                out_ref[d, x] = product[
                    x * thin : (x + 1) * thin, d * across_wide : (d + 1) * across_wide
                ]

    @pl.when(step == pl.num_programs(0) - 1)
    def _():
        total = total_ref[...]
        n, r = normalise(mid_ref[...])
        dmid = grad.read(rows, refs[:count]) + norm_backward(n, r, total, gain_ref[1:2, :])
        dmid_ref[...] = dmid
        gz = dmid.astype(BF16)
        datt_ref[...] = mm_nt(gz, wout_ref[...]).astype(BF16)
        sum_ref[...] = start_ref[...]
        add_norm_sums(2 * layer + 1, sum_ref, total, n)
        product = mm(att_ref[...], gz).astype(BF16)
        for own in range(2):

            @pl.when(core == own)
            def _(own=own):
                for s in range(slabs):
                    out_ref = up_kept if s % 2 == own else up_gone
                    for d in range(dp_size):
                        out_ref[d, s // 2, :, wide:] = product[
                            d * deep : (d + 1) * deep, s * thin : (s + 1) * thin
                        ]


def feed_backward(
    layer,
    grad,
    slope,
    active,
    mid,
    h,
    att_turned,
    gain,
    wdown,
    wup,
    wout,
    start,
    core,
    slabs,
    dp_size,
    after,
):
    rows, width = grad.rows, grad.width
    hidden = wup.shape[2]
    half = slabs // 2
    wide, thin = hidden // slabs, width // slabs
    chunk = max(wide, 768)
    down_wide = hidden // dp_size
    pair = chunk // down_wide

    def fixed(shape):
        return pl.BlockSpec(
            shape, lambda c, core: (0,) * len(shape), pipeline_mode=pl.Buffered(1)
        )

    def of_layer(stacked):
        rest = stacked.shape[1:]
        return pl.BlockSpec(
            (None,) + rest,
            lambda c, core: (layer,) + (0,) * len(rest),
            pipeline_mode=pl.Buffered(1),
        )

    by_chunk = pl.BlockSpec((rows, chunk), lambda c, core: (0, c))
    up_shape = (dp_size, half, width // dp_size, wide + thin)
    down_shape = (dp_size, half, thin, down_wide)
    down_spec = pl.BlockSpec((pair, half, thin, down_wide), lambda c, core: (c, 0, 0, 0))
    return pl.pallas_call(
        without(
            functools.partial(feed_back_kernel, layer, grad, dp_size),
            1 + grad.count() + 10,
            len(after),
        ),
        grid_spec=pltpu.PrefetchScalarGridSpec(
            num_scalar_prefetch=1,
            grid=(hidden // chunk,),
            in_specs=[fixed(operand.shape) for operand in grad.operands()]
            + [by_chunk, by_chunk]
            + [fixed(one.shape) for one in (mid, h, att_turned)]
            + [
                of_layer(gain),
                pl.BlockSpec((None, width, chunk), lambda c, core: (layer, 0, c)),
                pl.BlockSpec((None, chunk, width), lambda c, core: (layer, c, 0)),
                of_layer(wout),
                fixed(start.shape),
            ]
            + ordered(after),
            out_specs=[fixed(up_shape)] * 2
            + [down_spec] * 2
            + [fixed((rows, width))] * 2
            + [fixed(start.shape)],
            scratch_shapes=[
                pltpu.VMEM((rows, width), BF16),
                pltpu.VMEM((2, width // 2, rows), BF16),
                pltpu.VMEM((rows, width), F32),
            ],
        ),
        out_shape=[jax.ShapeDtypeStruct(up_shape, BF16)] * 2
        + [jax.ShapeDtypeStruct(down_shape, BF16)] * 2
        + [
            jax.ShapeDtypeStruct((rows, width), F32),
            jax.ShapeDtypeStruct((rows, width), BF16),
            jax.ShapeDtypeStruct(start.shape, F32),
        ],
        compiler_params=params(),
        cost_estimate=pl.CostEstimate(
            flops=4 * rows * width * (width + 2 * hidden),
            bytes_accessed=20 * rows * width + 4 * rows * hidden + 8 * width * hidden,
            transcendentals=0,
        ),
        name="feed_back",
    )(
        core,
        *grad.operands(),
        slope,
        active,
        mid,
        h,
        att_turned,
        gain,
        wup,
        wdown,
        wout,
        start,
        *after,
    )


def summed(refs):
    total = refs[0][...].astype(F32)
    for ref in refs[1:]:
        total += ref[...].astype(F32)
    return total.astype(BF16)


def joined(groups, parts, refs):
    dkv = [summed(refs[groups + g * parts : groups + (g + 1) * parts]) for g in range(groups)]
    pieces = [ref[...] for ref in refs[:groups]]
    pieces += [block[0] for block in dkv]
    pieces += [block[1] for block in dkv]
    return jnp.concatenate(pieces, axis=1)


def joined_specs(groups, parts, tile, width, offset=0):
    one = pl.BlockSpec((tile, width // groups), lambda i: (i + offset, 0))
    pair = pl.BlockSpec((2, tile, width // groups), lambda i: (0, i + offset, 0))
    return [one] * groups + [pair] * (groups * parts)


def qkv_grad_kernel(layer, groups, parts, x, tile, ends, core_ref, *refs):
    before = groups * (1 + parts)
    x_refs = refs[before : before + x.count()]
    gain_ref, w_ref, h_ref, dmid_ref, start_ref, species_ref = refs[before + x.count() :][:6]
    gone_ref, kept_ref, grad_ref, sum_ref, full_ref = refs[before + x.count() + 6 :]
    dp_size, half, deep, wide = gone_ref.shape
    step, steps = pl.program_id(0), pl.num_programs(0)
    full = joined(groups, parts, refs)
    full_ref[pl.ds(pl.multiple_of(step * tile, tile), tile), :] = full

    @pl.when(step == 0)
    def _():
        sum_ref[...] = start_ref[...]

    @pl.when(step < ends)
    def _():
        e = mm_nt(full, w_ref[...])
        n, r = normalise(x.read(tile, x_refs))
        grad = dmid_ref[...] + norm_backward(n, r, e, gain_ref[0:1, :])
        grad_ref[...] = grad.astype(grad_ref.dtype)
        add_norm_sums(2 * layer, sum_ref, e, n)
        if layer == 0:
            row = pl.ds(4 * LAYERS + species_ref[0], 1)
            sum_ref[row, :] += jnp.sum(grad, axis=0, keepdims=True)

    @pl.when(step == steps - 1)
    def _():
        first = h_ref.shape[1] // 2
        h = jnp.concatenate([h_ref[:, first:], h_ref[:, :first]], axis=1)
        for s in range(2 * half):
            product = mm(h, full_ref[:, s * wide : (s + 1) * wide]).astype(BF16)
            for own in range(2):

                @pl.when(core_ref[0] == own)
                def _(own=own, s=s, product=product):
                    out_ref = kept_ref if s % 2 == own else gone_ref
                    for d in range(dp_size):
                        out_ref[d, s // 2] = product[d * deep : (d + 1) * deep, :]


def qkv_gradients(
    layer, ends, kind, dq, dkv, x, gain, w, h, dmid, start, species, core, slabs, dp_size, after
):
    groups, parts = len(dq), len(dkv[0])
    rows, width = dmid.shape
    tile = min(256, rows // 2)
    tiles = rows // tile
    turn_to = tiles // 2
    half = slabs // 2
    shape = (dp_size, half, width // dp_size, 3 * width // slabs)

    def fixed(shape):
        return pl.BlockSpec(
            shape, lambda i, core: (0,) * len(shape), pipeline_mode=pl.Buffered(1)
        )

    def of_layer(stacked):
        rest = stacked.shape[1:]
        return pl.BlockSpec(
            (None,) + rest,
            lambda i, core: (layer,) + (0,) * len(rest),
            pipeline_mode=pl.Buffered(1),
        )

    def at(i):
        return lax.rem(i + turn_to, tiles)

    def used(i):
        return at(jnp.minimum(i, ends - 1))

    def out_at(i):
        return used(i) if ends == tiles else jnp.minimum(i, ends - 1)

    one = pl.BlockSpec((tile, width // groups), lambda i, core: (at(i), 0))
    both = pl.BlockSpec((2, tile, width // groups), lambda i, core: (0, at(i), 0))
    if ends == tiles:
        x_specs = [pl.BlockSpec((tile, width), lambda i, core: (used(i), 0))]
    else:
        x_specs = [pl.BlockSpec((tile, width), lambda i, core: (out_at(i), 0))]
    if x.shift is not None:
        x_specs.append(fixed((1, width)))
    return pl.pallas_call(
        without(
            functools.partial(qkv_grad_kernel, layer, groups, parts, x, tile, ends),
            1 + groups * (1 + parts) + x.count() + 6,
            len(after),
        ),
        grid_spec=pltpu.PrefetchScalarGridSpec(
            num_scalar_prefetch=1,
            grid=(tiles,),
            in_specs=[one] * groups
            + [both] * (groups * parts)
            + x_specs
            + [of_layer(gain), of_layer(w), fixed(h.shape)]
            + [pl.BlockSpec((tile, width), lambda i, core: (used(i), 0)), fixed(start.shape)]
            + [pl.BlockSpec(memory_space=pltpu.SMEM)]
            + ordered(after),
            out_specs=[fixed(shape)] * 2
            + [pl.BlockSpec((tile, width), lambda i, core: (out_at(i), 0)), fixed(start.shape)],
            scratch_shapes=[pltpu.VMEM((rows, 3 * width), BF16)],
        ),
        out_shape=[jax.ShapeDtypeStruct(shape, BF16)] * 2
        + [
            jax.ShapeDtypeStruct((ends * tile, width), kind),
            jax.ShapeDtypeStruct(start.shape, F32),
        ],
        compiler_params=params(),
        cost_estimate=pl.CostEstimate(
            flops=12 * rows * width * width, bytes_accessed=32 * rows * width, transcendentals=0
        ),
        name="qkv_grad",
    )(
        core,
        *dq,
        *[block for group in dkv for block in group],
        *x.operands(),
        gain,
        w,
        h,
        dmid,
        start,
        species,
        *after,
    )


def qkv_back_kernel(layer, groups, parts, x, tile, *refs):
    before = groups * (1 + parts)
    gain_ref, w_ref, dmid_ref, start_ref, species_ref = refs[before + x.count() :][:5]
    grad_ref, sum_ref = refs[before + x.count() + 5 :]
    full = joined(groups, parts, refs)
    e = mm_nt(full, w_ref[...])
    n, r = normalise(x.read(tile, refs[before : before + x.count()]))
    grad = dmid_ref[...] + norm_backward(n, r, e, gain_ref[0:1, :])
    grad_ref[...] = grad.astype(grad_ref.dtype)

    @pl.when(pl.program_id(0) == 0)
    def _():
        sum_ref[...] = start_ref[...]

    add_norm_sums(2 * layer, sum_ref, e, n)
    if layer == 0:
        row = pl.ds(4 * LAYERS + species_ref[0], 1)
        sum_ref[row, :] += jnp.sum(grad, axis=0, keepdims=True)


def qkv_backward(layer, first_row, kind, dq, dkv, x, gain, w, dmid, start, species, after):
    groups, parts = len(dq), len(dkv[0])
    rows, width = x.rows, x.width
    tile = min(256, dmid.shape[0] // 2)
    offset = first_row // tile
    sums = pl.BlockSpec(start.shape, lambda i: (0, 0))
    return pl.pallas_call(
        without(
            functools.partial(qkv_back_kernel, layer, groups, parts, x, tile),
            groups * (1 + parts) + x.count() + 5,
            len(after),
        ),
        grid=(rows // tile,),
        in_specs=joined_specs(groups, parts, tile, width, offset)
        + x.specs(tile)
        + [layer_of(gain, layer), layer_of(w, layer)]
        + [pl.BlockSpec((tile, width), lambda i: (i + offset, 0)), sums]
        + [pl.BlockSpec(memory_space=pltpu.SMEM)]
        + ordered(after),
        out_specs=[rows_of(tile, width), sums],
        out_shape=[
            jax.ShapeDtypeStruct((rows, width), kind),
            jax.ShapeDtypeStruct(start.shape, F32),
        ],
        compiler_params=params(),
        cost_estimate=pl.CostEstimate(
            flops=6 * rows * width * width, bytes_accessed=24 * rows * width, transcendentals=0
        ),
        name="qkv_back",
    )(
        *dq,
        *[block for group in dkv for block in group],
        *x.operands(),
        gain,
        w,
        dmid,
        start,
        species,
        *after,
    )


def token_of(ref):
    ref[...] = jnp.zeros_like(ref)


TOKEN = jax.ShapeDtypeStruct((8, 128), F32)


def place_kernel(mine_ref, own_ref, came_ref, out_ref, token_ref):
    token_of(token_ref)
    mine = pl.program_id(0) == mine_ref[0]
    out_ref[...] = jnp.where(mine, own_ref[...], came_ref[...].astype(F32))


def place_cells(mine, value, came):
    rows, width = came.shape
    tile = min(256, rows)
    spec = pl.BlockSpec((tile, width), lambda c, i, mine: (i, 0))
    return pl.pallas_call(
        place_kernel,
        grid_spec=pltpu.PrefetchScalarGridSpec(
            num_scalar_prefetch=1,
            grid=(2, rows // tile),
            in_specs=[spec, spec],
            out_specs=[
                pl.BlockSpec((None, tile, width), lambda c, i, mine: (c, i, 0)),
                pl.BlockSpec(TOKEN.shape, lambda c, i, mine: (0, 0)),
            ],
        ),
        out_shape=[jax.ShapeDtypeStruct((2, rows, width), F32), TOKEN],
        compiler_params=params(16),
        cost_estimate=pl.CostEstimate(
            flops=rows * width, bytes_accessed=20 * rows * width, transcendentals=0
        ),
        name="place_cells",
    )(mine, value, came)


class Sum:
    def __init__(self, came, kept, steps, sizes, places, layer, results, scatter, part=(0, 1)):
        self.part = part
        self.whole = True
        self.sizes = sizes
        self.places = places
        self.scatter = scatter
        self.left = {
            "blk": bits_of(sizes["blk"])[1:],
            "dp": bits_of(sizes["dp"]),
        }
        self.steps = [step for step in steps if not scatter or step[0] == "blk"]
        self.layer = layer
        self.results = results
        self.kept = kept
        self.came = came
        self.over_blk = False
        self.waiting = 0
        self.finished = False

    def ready(self):
        ends = not (self.scatter or self.over_blk or self.steps)
        return not ends or self.layer == LAYERS - 1 or bool(self.results.held)

    def spread(self, call, outer, inner, tail):
        by_outer, by_inner = math.gcd(call.count, outer), math.gcd(call.count, inner)
        if by_outer >= by_inner:
            by = by_outer
            return (outer // by, 1, inner) + tail, lambda j, side: (
                j // (call.count // by),
                side,
                0,
                0,
                0,
            )
        by = by_inner
        return (outer, 1, inner // by) + tail, lambda j, side: (
            0,
            side,
            j // (call.count // by),
            0,
            0,
        )

    def prepare_scatter(self, call):
        tail = self.kept.shape[-2:]
        shape = (math.prod(self.kept.shape[:-2]), 1, 1) + tail
        block, index = self.spread(call, shape[0], 1, tail)
        spec = pl.BlockSpec(block, lambda j, side: index(j, 0))
        reads = [call.read(one.reshape(shape), spec) for one in (self.kept, self.came)]
        write = call.write(shape, BF16, spec)

        def work(refs):
            refs[write][...] = refs[reads[0]][...] + refs[reads[1]][...]

        def finish(out):
            whole = out(write).reshape((self.sizes["dp"], -1) + tail)
            self.kept = lax.psum_scatter(whole, "dp", scatter_dimension=0, tiled=False)
            self.came = None
            self.left = {"blk": [], "dp": []}
            self.steps = []
            self.waiting = self.scatter
            self.scatter = 0
            self.over_blk = True

        return work, finish

    def prepare_over_blk(self, call):
        at = call.carry(self.kept)

        def finish(out):
            blk = self.sizes["blk"]
            cores = [list(range(core, blk, 2)) for core in range(2)]
            self.kept = lax.psum_scatter(
                out(at), "blk", scatter_dimension=0, axis_index_groups=cores, tiled=False
            )
            self.over_blk = False
            self.waiting = 2

        return (lambda refs: None), finish

    def prepare(self, call):
        if self.scatter:
            return self.prepare_scatter(call)
        if self.over_blk:
            return self.prepare_over_blk(call)
        if not self.steps:
            return self.prepare_last(call)
        axis, bit = self.steps[0]
        at = self.left[axis].index(bit)
        inner = 1 << at
        if axis == "dp":
            inner <<= len(self.left["blk"])
        total = 1 << (len(self.left["blk"]) + len(self.left["dp"]))
        outer = total // (2 * inner)
        tail = self.kept.shape[-2:]
        shape = (outer, 2, inner) + tail
        piece = 0
        if self.whole:
            piece = self.part[0]
            tail = (tail[0] // self.part[1], tail[1])
        block, index = self.spread(call, outer, inner, tail)
        side = (self.places[axis] // bit) % 2
        sources = [self.kept.reshape(shape)]
        if self.came is not None:
            sources.append(self.came.reshape(shape))
        reads = []
        for value in (1 - side, side):
            at = call.scalar(value)
            spec = pl.BlockSpec(
                block, lambda j, side, at=at: index(j, side[at])[:3] + (piece, 0)
            )
            reads.append([call.read(one, spec) for one in sources])
        spec = pl.BlockSpec(block, lambda j, side: index(j, 0))
        writes = [call.write((outer, 1, inner) + tail, BF16, spec) for _ in range(2)]

        def work(refs):
            for some, write in zip(reads, writes):
                values = [refs[i][...] for i in some]
                refs[write][...] = values[0] if len(values) == 1 else values[0] + values[1]

        def finish(out):
            self.steps.pop(0)
            self.left[axis].remove(bit)
            self.whole = False
            self.kept = out(writes[1])
            self.came = exchange(out(writes[0]), axis, self.sizes[axis], bit)

        return work, finish

    def prepare_last(self, call):
        rows, wide = self.kept.shape[-2:]
        spec = pl.BlockSpec((rows, wide), lambda j, side: (0, 0))
        sources = [one for one in (self.kept, self.came) if one is not None]
        reads = [call.read(one.reshape(rows, wide), spec) for one in sources]
        writes = []
        first, count = self.part
        for name, columns in self.results.names:
            block = (rows * count, columns)
            spec = pl.BlockSpec((None,) + block, lambda j, side: (self.layer, 0, 0))
            if name not in call.shared:
                held = self.results.held.get(name)
                call.shared[name] = call.write((LAYERS,) + block, F32, spec, held)
            writes.append(call.shared[name])

        def work(refs):
            total = refs[reads[0]][...].astype(F32)
            if len(reads) == 2:
                total += refs[reads[1]][...].astype(F32)
            at = 0
            for write, (_, columns) in zip(writes, self.results.names):
                refs[write][first * rows : (first + 1) * rows, :] = total[:, at : at + columns]
                at += columns

        def finish(out):
            self.finished = True
            for write, (name, _) in zip(writes, self.results.names):
                self.results.held[name] = out(write)

        return work, finish


class Results:
    def __init__(self, names):
        self.names = names
        self.held = {}


class SmallSum:
    def __init__(self, value, sizes):
        self.value = value
        self.sizes = sizes
        self.steps = []
        for axis in ("blk", "dp"):
            bits = bits_of(sizes[axis])
            apart = len(bits) - 2 if axis == "dp" and len(bits) > 2 else len(bits)
            self.steps += [(axis, (bit,)) for bit in bits[:apart]]
            if apart < len(bits):
                first, second = bits[apart:]
                self.steps.append((axis, (first, second, first + second)))
        self.came = None
        self.waiting = 0
        self.finished = False
        self.send()

    def ready(self):
        return True

    def send(self):
        axis, masks = self.steps.pop(0)
        self.came = [exchange(self.value, axis, self.sizes[axis], mask) for mask in masks]

    def prepare(self, call):
        shape = self.value.shape
        spec = pl.BlockSpec(shape, lambda j, side: (0, 0))
        reads = [call.read(one, spec) for one in [self.value] + self.came]
        if self.steps:
            writes = [call.write(shape, F32, spec)]
        else:
            norms = (LAYERS, 2, shape[1])
            spec = pl.BlockSpec(norms, lambda j, side: (0, 0, 0))
            writes = [call.write(norms, F32, spec) for _ in range(2)]
            spec = pl.BlockSpec((2, shape[1]), lambda j, side: (0, 0))
            writes.append(call.write((2, shape[1]), F32, spec))
        last = not self.steps

        def work(refs):
            values = [refs[i][...] for i in reads]
            while len(values) > 1:
                values = [a + b for a, b in zip(values[::2], values[1::2])]
            if not last:
                refs[writes[0]][...] = values[0]
                return
            for which in range(2):
                for row in range(2 * LAYERS):
                    at = which * 2 * LAYERS + row
                    refs[writes[which]][row // 2, row % 2 : row % 2 + 1, :] = values[0][
                        at : at + 1, :
                    ]
            refs[writes[2]][...] = values[0][4 * LAYERS : 4 * LAYERS + 2, :]

        def finish(out):
            if last:
                self.value = [out(write) for write in writes]
                self.finished = True
            else:
                self.value = out(writes[0])
                self.send()

        return work, finish


class Call:
    def __init__(self):
        self.count = 2
        self.scalars, self.operands, self.in_specs = [], [], []
        self.out_specs, self.shapes, self.held = [], [], []
        self.shared = {}

    def scalar(self, value):
        self.scalars.append(value)
        return len(self.scalars) - 1

    def read(self, operand, spec):
        self.operands.append(operand)
        self.in_specs.append(spec)
        return ("in", len(self.operands) - 1)

    def write(self, shape, kind, spec, held=None):
        self.shapes.append(jax.ShapeDtypeStruct(shape, kind))
        self.out_specs.append(spec)
        self.held.append(held)
        return ("out", len(self.shapes) - 1)

    def carry(self, operand):
        spec = pl.BlockSpec(memory_space=pl.ANY)
        return self.write(operand.shape, operand.dtype, spec, operand)


def fold(moving, after, passed=(), at_end=False):
    call = Call()
    call.scalar(jnp.int32(0))
    tasks = []
    for one in moving:
        if one.waiting:
            one.waiting -= 1
        elif one.ready():
            tasks.append(one.prepare(call))
    if not tasks:
        return after[0], passed
    token = call.write(
        TOKEN.shape, TOKEN.dtype, pl.BlockSpec(TOKEN.shape, lambda j, side: (0, 0))
    )
    tasks.append((lambda refs: token_of(refs[token]), lambda out: None))
    spare = pl.BlockSpec(memory_space=pl.ANY)
    kept_back = [(i, one) for i, one in enumerate(call.held) if one is not None]
    for array in passed:
        kept_back.append((len(call.shapes), array))
        call.shapes.append(jax.ShapeDtypeStruct(array.shape, array.dtype))
        call.out_specs.append(spare)
    inputs = len(call.operands)
    unused = len(kept_back) + len(after)

    def kernel(side_ref, *refs):
        where = {}
        for i in range(inputs):
            where[("in", i)] = refs[i]
        for i in range(len(call.shapes)):
            where[("out", i)] = refs[inputs + unused + i]
        for work, _ in tasks:
            work(where)

    size = sum(math.prod(shape.shape) for shape in call.shapes)
    out = pl.pallas_call(
        kernel,
        grid_spec=pltpu.PrefetchScalarGridSpec(
            num_scalar_prefetch=1,
            grid=(call.count,),
            in_specs=call.in_specs + [spare] * unused,
            out_specs=call.out_specs,
        ),
        out_shape=call.shapes,
        input_output_aliases={1 + inputs + i: at for i, (at, _) in enumerate(kept_back)},
        compiler_params=params(16 if at_end else 64),
        cost_estimate=pl.CostEstimate(flops=size, bytes_accessed=6 * size, transcendentals=0),
        name="fold",
    )(
        jnp.stack(call.scalars).astype(jnp.int32),
        *call.operands,
        *[array for _, array in kept_back],
        *after,
    )
    for _, finish in tasks:
        finish(lambda write: out[write[1]])
    moving[:] = [one for one in moving if not one.finished]
    return out[token[1]], tuple(out[len(out) - len(passed) :])


def exchange(value, axis, size, bit):
    return lax.ppermute(value, axis, [(i, i ^ bit) for i in range(size)])


def bits_of(size):
    return [1 << i for i in range(size.bit_length() - 1)]


def shards(
    dp_size,
    blk_size,
    embedded,
    species_flag,
    gene_ids,
    species_table,
    norm_gain,
    norm_bias,
    w_qkv,
    w_out,
    w_up,
    w_down,
    out_cotangent,
):
    _, block_len, width = embedded.shape
    half = blk_size // 2
    place = lax.axis_index("blk")
    mine = place // half

    def swap(value):
        return exchange(value, "blk", blk_size, half)

    def own_and_other(pair):
        first = mine == 0
        return jnp.where(first, pair[0], pair[1]), jnp.where(first, pair[1], pair[0])

    def collect(pair):
        own, other = own_and_other(pair)
        return own, swap(other)

    def turn(value, by):
        pairs = []
        for b in range(blk_size):
            base, j = b // half * half, b % half
            pairs.append((b, base + (j - by) % half))
        return lax.ppermute(value, "blk", pairs)

    def gather_parts(value):
        return [value] + [turn(value, by) for by in range(1, half)]

    ids = jnp.concatenate(collect(gene_ids))
    dead = jnp.where(ids != 0, 0.0, MASKED).astype(BF16)
    dead_parts = [
        jnp.broadcast_to(part[:, None], (part.shape[0], PAIR)) for part in gather_parts(dead)
    ]
    species, _ = own_and_other(species_flag)
    picked = jnp.where(species == 0, species_table[0], species_table[1])
    state = Tokens(collect(embedded), picked[None, :])
    cotangent = Tokens(collect(out_cotangent))

    kept = []
    for layer in range(LAYERS):
        first = tuple(dead_parts) if layer == 0 else ()
        h1, q, kv = qkv_forward(layer, state, norm_gain, norm_bias, w_qkv, first)
        kv_parts = gather_parts(kv)
        att, inverse, p = attend(q, kv_parts, dead_parts)
        mid, h2, att_turned, active, slope, after = feed_forward(
            layer, att, state, w_out, norm_gain, norm_bias, w_up, w_down
        )
        kept.append(
            (state, h1, q, kv_parts, att, inverse, p, mid, h2, att_turned, active, slope)
        )
        state = Tokens([after])
    came = swap(after[block_len:].astype(BF16))
    hidden_out, placed = place_cells(mine[None], after, came)

    sizes = {"blk": blk_size, "dp": dp_size}
    places = {"blk": place, "dp": lax.axis_index("dp")}
    core = place % 2
    over_blk = [("blk", bit) for bit in bits_of(blk_size)[1:]]
    over_dp = [("dp", bit) for bit in bits_of(dp_size)]
    core = core[None]

    def column_sums(pair, orders, layer, results, waits):
        gone, own = (value.reshape((half * dp_size,) + value.shape[-2:]) for value in pair)
        came = exchange(gone, "blk", blk_size, 1)
        scatter = waits if layer > 0 else 0
        if own.shape[1] % (16 * len(orders)):
            orders = orders[:1]
        return [
            Sum(came, own, order, sizes, places, layer, results, scatter, (i, len(orders)))
            for i, order in enumerate(orders)
        ]

    up_width = w_up.shape[2] // blk_size
    of_up_out = Results([("up", up_width), ("out", width // blk_size)])
    of_down = Results([("down", w_down.shape[1] // dp_size)])
    of_qkv = Results([("qkv", 3 * width // blk_size)])
    groups = 2
    grad = cotangent
    moving = []
    last = ()
    small = jnp.zeros((16, width), F32)
    species = species[None]
    for layer in reversed(range(LAYERS)):
        x, h1, q, kv_parts, att, inverse, p, mid, h2, att_turned, active, slope = kept[layer]
        up_gone, up_kept, down_gone, down_kept, dmid, datt, small = feed_backward(
            layer,
            grad,
            slope,
            active,
            mid,
            h2,
            att_turned,
            norm_gain,
            w_down,
            w_up,
            w_out,
            small,
            core,
            blk_size,
            dp_size,
            last,
        )
        last = (datt,)
        if moving:
            added, _ = fold(moving, last)
            last = (added,)
        moving += column_sums((up_gone, up_kept), [over_blk + over_dp], layer, of_up_out, 3)
        moving += column_sums((down_gone, down_kept), [over_dp + over_blk], layer, of_down, 3)
        arrived = (came,)
        dq, dkv = [], []
        for group in range(groups):
            one_dq, one_dkv = attend_back(
                group, groups, q, inverse, att, datt, p, kv_parts, last
            )
            others = tuple(one_dkv[1:])
            if group == groups - 1:
                added, others = fold(moving, (one_dq,) + arrived, others)
            else:
                added, _ = fold(moving, (one_dq,) + arrived)
            arrived = tuple(turn(value, half - 1 - by) for by, value in enumerate(others))
            last = (added,)
            dq.append(one_dq)
            dkv.append((one_dkv[0],) + arrived)
        if layer > 0:
            orders = [over_dp + over_blk]
        else:
            near, far = over_dp[:1], over_dp[1:]
            orders = [near + over_blk + far, far[:1] + near + over_blk + far[1:]]
        tiles = 2 * block_len // min(256, block_len)
        ends = tiles if layer > 0 else tiles // 2
        moved = x if layer > 0 else Tokens([x.arrays[1]], x.shift)
        gone, own, one_grad, small = qkv_gradients(
            layer,
            ends,
            F32 if layer > 0 else BF16,
            dq,
            dkv,
            moved,
            norm_gain,
            w_qkv,
            h1,
            dmid,
            small,
            species,
            core,
            blk_size,
            dp_size,
            last,
        )
        if layer == 0:
            added, (one_grad, gone) = fold(moving, (own,), (one_grad, gone))
            last = (added,)
        moving += column_sums((gone, own), orders, layer, of_qkv, 0)
        if layer > 0:
            last = (one_grad,)
            grad = Tokens([one_grad])
        else:
            came = swap(one_grad)
            own_x = Tokens([x.arrays[0]], x.shift)
            own_grad, small = qkv_backward(
                layer, 0, F32, dq, dkv, own_x, norm_gain, w_qkv, dmid, small, species, last
            )
            added, (small,) = fold(moving, (own_grad, came), (small,))
            last = (added,)
    small = SmallSum(small, sizes)
    moving.append(small)
    embed_grad, embed_placed = place_cells(mine[None], own_grad, came)
    last += (placed, embed_placed)
    while moving:
        added, _ = fold(moving, last, (), True)
        last = (added,)

    gain_grad, bias_grad, species_grad = small.value
    return (
        hidden_out,
        embed_grad,
        species_grad,
        gain_grad,
        bias_grad,
        of_qkv.held["qkv"],
        of_up_out.held["out"],
        of_up_out.held["up"],
        of_down.held["down"].transpose(0, 2, 1),
    )


def solution(mesh):
    placed = (
        P("dp", "blk", None),
        P("dp"),
        P("dp", "blk"),
        P(),
        P(),
        P(),
        P(),
        P(),
        P(),
        P(),
        P("dp", "blk", None),
    )
    return jax.shard_map(
        functools.partial(shards, mesh.shape["dp"], mesh.shape["blk"]),
        mesh=mesh,
        in_specs=placed,
        out_specs=(
            P("dp", "blk", None),
            P("dp", "blk", None),
            P(),
            P(),
            P(),
            P(None, "dp", "blk"),
            P(None, "dp", "blk"),
            P(None, "dp", "blk"),
            P(None, "dp", "blk"),
        ),
        check_vma=False,
    )
```

```python
import functools
import math

import jax
import jax.numpy as jnp
from jax import lax
from jax.experimental import pallas as pl
from jax.experimental.pallas import tpu as pltpu
from jax.sharding import PartitionSpec as P

HEADS = 12
HEAD_DIM = 64
LAYERS = 2
PAIR = 2 * HEAD_DIM
EPS = 1e-05
LOG2E = 1.4426950408889634
LN2 = 0.6931471805599453
SCALE = 1.0 / math.sqrt(HEAD_DIM)
MASKED = -1e30
MIB = 1024 * 1024

F32 = jnp.float32
BF16 = jnp.bfloat16


def mm(left, right):
    return jnp.dot(left, right, preferred_element_type=F32)


def mm_nt(left, right):
    return lax.dot_general(left, right, (((1,), (1,)), ((), ())), preferred_element_type=F32)


def mm_tn(left, right):
    return lax.dot_general(left, right, (((0,), (0,)), ((), ())), preferred_element_type=F32)


def pieced(product, left, right, axis):
    wide = right.shape[axis]
    pieces = [
        product(
            left[...],
            right[:, at : min(at + 256, wide)]
            if axis == 1
            else right[at : min(at + 256, wide), :],
        )
        for at in range(0, wide, 256)
    ]
    return pieces[0] if len(pieces) == 1 else jnp.concatenate(pieces, axis=1)


def normalise(value):
    mean = jnp.mean(value, axis=-1, keepdims=True)
    centred = value - mean
    variance = jnp.mean(centred * centred, axis=-1, keepdims=True)
    r = lax.rsqrt(variance + EPS)
    return centred * r, r


def norm_backward(n, r, e, gain):
    eg = e * gain
    first = jnp.mean(eg, axis=-1, keepdims=True)
    second = jnp.mean(eg * n, axis=-1, keepdims=True)
    return r * (eg - first - n * second)


def params(mib=64):
    return pltpu.CompilerParams(vmem_limit_bytes=mib * MIB)


def whole(shape):
    return pl.BlockSpec(shape, lambda i: (0,) * len(shape), pipeline_mode=pl.Buffered(1))


def rows_of(tile, width):
    return pl.BlockSpec((tile, width), lambda i: (i, 0))


def slabs_of(count, tile, width):
    return pl.BlockSpec((count, tile, width), lambda i: (0, i, 0))


def columns_of(width, tile):
    return pl.BlockSpec((width, tile), lambda i: (0, i))


def layer_of(stacked, layer):
    rest = stacked.shape[1:]
    return pl.BlockSpec(
        (None,) + rest, lambda i: (layer,) + (0,) * len(rest), pipeline_mode=pl.Buffered(1)
    )


def ordered(after):
    return [pl.BlockSpec(memory_space=pl.ANY)] * len(after)


def without(kernel, first, count):
    def run(*refs):
        return kernel(*refs[:first], *refs[first + count :])

    return run


def turned(value):
    return value.T.astype(BF16)


class Tokens:
    def __init__(self, arrays, shift=None):
        self.arrays = arrays
        self.shift = shift
        self.rows = sum(array.shape[0] for array in arrays)
        self.width = arrays[0].shape[1]

    def operands(self):
        return list(self.arrays) + ([] if self.shift is None else [self.shift])

    def specs(self, tile):
        tiles = self.arrays[0].shape[0] // tile
        if len(self.arrays) == 1:
            specs = [rows_of(tile, self.width)]
        else:
            specs = [
                pl.BlockSpec((tile, self.width), lambda i: (jnp.minimum(i, tiles - 1), 0)),
                pl.BlockSpec((tile, self.width), lambda i: (jnp.maximum(i - tiles, 0), 0)),
            ]
        return specs + ([] if self.shift is None else [whole((1, self.width))])

    def count(self):
        return len(self.operands())

    def read(self, tile, refs):
        value = refs[0][...].astype(F32)
        if tile == self.rows and len(self.arrays) == 2:
            value = jnp.concatenate([value, refs[1][...].astype(F32)], axis=0)
        elif len(self.arrays) == 2:
            first = pl.program_id(0) < self.arrays[0].shape[0] // tile
            value = jnp.where(first, value, refs[1][...].astype(F32))
        return value if self.shift is None else value + refs[-1][...]


def qkv_kernel(x, tile, *refs):
    gain_ref, bias_ref, w_ref, h_ref, q_ref, kv_ref = refs[x.count() :]
    width = x.width
    n, _ = normalise(x.read(tile, refs[: x.count()]))
    h = n * gain_ref[0:1, :] + bias_ref[0:1, :]
    h_ref[...] = turned(h)
    h = h.astype(BF16)
    kv_ref[...] = mm(h, w_ref[:, width:]).astype(BF16)
    q_ref[...] = (mm(h, w_ref[:, :width]) * (SCALE * LOG2E)).astype(BF16)


def qkv_forward(layer, x, gain, bias, w, after):
    rows, width = x.rows, x.width
    tile = min(256, rows // 2)
    return pl.pallas_call(
        without(functools.partial(qkv_kernel, x, tile), x.count() + 3, len(after)),
        grid=(rows // tile,),
        in_specs=x.specs(tile)
        + [layer_of(value, layer) for value in (gain, bias, w)]
        + ordered(after),
        out_specs=[columns_of(width, tile), rows_of(tile, width), rows_of(tile, 2 * width)],
        out_shape=[
            jax.ShapeDtypeStruct((width, rows), BF16),
            jax.ShapeDtypeStruct((rows, width), BF16),
            jax.ShapeDtypeStruct((rows, 2 * width), BF16),
        ],
        compiler_params=params(),
        cost_estimate=pl.CostEstimate(
            flops=6 * rows * width * width, bytes_accessed=12 * rows * width, transcendentals=0
        ),
        name="norm_qkv",
    )(*x.operands(), gain, bias, w, *after)


def lanes_like(shape):
    lane = lax.broadcasted_iota(jnp.int32, shape, 1)
    return lane < HEAD_DIM, lane & (HEAD_DIM - 1)


def three_parts(value, sub, fourth):
    high = value.astype(BF16).astype(F32)
    rest = value - high
    middle = rest.astype(BF16).astype(F32)
    least = rest - middle
    return jnp.where(
        sub == 0,
        high,
        jnp.where(sub == 1, middle, jnp.where(sub == 2, least, jnp.where(sub == 3, fourth, 0.0))),
    )


def attend_kernel(parts, *refs):
    q_ref = refs[0]
    k_refs = refs[1 : 1 + parts]
    v_refs = refs[1 + parts : 1 + 2 * parts]
    dead_refs = refs[1 + 2 * parts : 1 + 3 * parts]
    o_ref, inverse_ref, p_ref, ka, kb, va, vb = refs[1 + 3 * parts :]
    rows = k_refs[0].shape[0]

    @pl.when(pl.program_id(1) == 0)
    def _():
        low, sub = lanes_like((rows, PAIR))
        for part in range(parts):
            own = slice(part * rows, (part + 1) * rows)
            k = k_refs[part][...].astype(F32)
            v = v_refs[part][...].astype(F32)
            extra = jnp.where(sub == 3, dead_refs[part][...].astype(F32), 0.0)
            ka[own, :] = jnp.where(low, k, extra).astype(BF16)
            kb[own, :] = jnp.where(low, extra, k).astype(BF16)
            va[:, own] = turned(jnp.where(low, v, 1.0))
            vb[:, own] = turned(jnp.where(low, 1.0, v))

    low, sub = lanes_like(q_ref.shape)
    fourth = jnp.where(sub == 3, 1.0, 0.0)
    q = q_ref[...].astype(F32)
    sa = mm_nt(jnp.where(low, q, fourth).astype(BF16), ka[...])
    sb = mm_nt(jnp.where(low, fourth, q).astype(BF16), kb[...])
    pa = jnp.exp2(sa - jnp.max(sa, axis=-1, keepdims=True)).astype(BF16)
    p_ref[0] = pa
    oa = mm_nt(va[...], pa)
    pb = jnp.exp2(sb - jnp.max(sb, axis=-1, keepdims=True)).astype(BF16)
    p_ref[1] = pb
    ob = mm_nt(vb[...], pb)
    inverse_a = 1.0 / oa[HEAD_DIM:, :]
    inverse_b = 1.0 / ob[:HEAD_DIM, :]
    value = jnp.concatenate([oa[:HEAD_DIM, :] * inverse_a, ob[HEAD_DIM:, :] * inverse_b], axis=0)
    inverse_ref[...] = jnp.concatenate([inverse_a, inverse_b], axis=0).T
    o_ref[...] = turned(value)


def attend(q, kv_parts, dead_parts):
    rows, width = q.shape
    parts = len(kv_parts)
    pairs = width // PAIR
    tile = min(512, rows)
    keys = parts * rows
    some = pl.BlockSpec((tile, PAIR), lambda j, i: (i, j))
    first = pl.BlockSpec((rows, PAIR), lambda j, i: (0, j))
    second = pl.BlockSpec((rows, PAIR), lambda j, i: (0, pairs + j))
    fixed = pl.BlockSpec((rows, PAIR), lambda j, i: (0, 0))
    scratch = pltpu.VMEM((keys, PAIR), BF16)
    turned_scratch = pltpu.VMEM((PAIR, keys), BF16)
    return pl.pallas_call(
        functools.partial(attend_kernel, parts),
        grid=(pairs, rows // tile),
        in_specs=[some] + [first] * parts + [second] * parts + [fixed] * parts,
        out_specs=[some, some, pl.BlockSpec((2, tile, keys), lambda j, i: (j, i, 0))],
        out_shape=[
            jax.ShapeDtypeStruct((rows, width), BF16),
            jax.ShapeDtypeStruct((rows, width), F32),
            jax.ShapeDtypeStruct((2 * pairs, rows, keys), BF16),
        ],
        scratch_shapes=[scratch] * 2 + [turned_scratch] * 2,
        compiler_params=params(),
        cost_estimate=pl.CostEstimate(
            flops=16 * rows * keys * width,
            bytes_accessed=4 * pairs * rows * keys,
            transcendentals=HEADS * rows * keys,
        ),
        name="attend",
    )(q, *kv_parts, *kv_parts, *dead_parts)


def attend_back_kernel(parts, *refs):
    q_ref, inverse_ref, att_ref, datt_ref, p_ref = refs[:5]
    k_refs = refs[5 : 5 + parts]
    v_refs = refs[5 + parts : 5 + 2 * parts]
    rest = refs[5 + 2 * parts :]
    dq_ref = rest[0]
    dkv_refs = rest[1 : 1 + parts]
    ks, va, vb, dk_turned, dv_turned = rest[1 + parts :]
    rows = k_refs[0].shape[0]
    index = pl.program_id(1)

    @pl.when(index == 0)
    def _():
        low, sub = lanes_like((rows, PAIR))
        ones = jnp.where(sub < 3, 1.0, 0.0)
        for part in range(parts):
            own = slice(part * rows, (part + 1) * rows)
            ks[:, own] = turned(k_refs[part][...].astype(F32))
            v = v_refs[part][...].astype(F32)
            va[own, :] = jnp.where(low, v, ones).astype(BF16)
            vb[own, :] = jnp.where(low, ones, v).astype(BF16)
        dk_turned[...] = jnp.zeros_like(dk_turned)
        dv_turned[...] = jnp.zeros_like(dv_turned)

    low, sub = lanes_like(q_ref.shape)
    q_turned = turned(q_ref[...].astype(F32))
    datt = datt_ref[...].astype(F32) * inverse_ref[...]
    datt_turned = turned(datt)
    product = datt * att_ref[...].astype(F32)
    term_a = jnp.sum(jnp.where(low, product, 0.0), axis=-1, keepdims=True)
    term_b = jnp.sum(jnp.where(low, 0.0, product), axis=-1, keepdims=True)
    extra = three_parts(-jnp.where(low, term_b, term_a), sub, 0.0)
    ta = mm_nt(jnp.where(low, datt, extra).astype(BF16), va[...])
    tb = mm_nt(jnp.where(low, extra, datt).astype(BF16), vb[...])
    first, second = slice(0, HEAD_DIM), slice(HEAD_DIM, PAIR)
    pa, pb = p_ref[0], p_ref[1]
    dv_turned[first, :] += mm(datt_turned[first, :], pa)
    ga = (pa.astype(F32) * ta).astype(BF16)
    dqa = mm_nt(ks[first, :], ga)
    dk_turned[first, :] += mm(q_turned[first, :], ga)
    dv_turned[second, :] += mm(datt_turned[second, :], pb)
    gb = (pb.astype(F32) * tb).astype(BF16)
    dqb = mm_nt(ks[second, :], gb)
    dk_turned[second, :] += mm(q_turned[second, :], gb)
    dq_ref[...] = turned(jnp.concatenate([dqa, dqb], axis=0) * SCALE)

    @pl.when(index == pl.num_programs(1) - 1)
    def _():
        for part in range(parts):
            own = slice(part * rows, (part + 1) * rows)
            dkv_refs[part][0] = (dk_turned[:, own].T * LN2).astype(BF16)
            dkv_refs[part][1] = dv_turned[:, own].T.astype(BF16)


def attend_back(group, groups, q, inverse, att, datt, p, kv_parts, after):
    rows, width = q.shape
    parts = len(kv_parts)
    pairs = width // PAIR
    count = pairs // groups
    base = group * count
    tile = min(512, rows)
    keys = parts * rows
    some = pl.BlockSpec((tile, PAIR), lambda j, i: (i, base + j))
    first = pl.BlockSpec((rows, PAIR), lambda j, i: (0, base + j))
    second = pl.BlockSpec((rows, PAIR), lambda j, i: (0, pairs + base + j))
    both = pl.BlockSpec((2, rows, PAIR), lambda j, i: (0, 0, j))
    all_keys = pltpu.VMEM((keys, PAIR), BF16)
    turned_keys = pltpu.VMEM((PAIR, keys), F32)
    out = pl.pallas_call(
        without(functools.partial(attend_back_kernel, parts), 5 + 2 * parts, len(after)),
        grid=(count, rows // tile),
        in_specs=[some] * 4
        + [pl.BlockSpec((2, tile, keys), lambda j, i: (base + j, i, 0))]
        + [first] * parts
        + [second] * parts
        + ordered(after),
        out_specs=[pl.BlockSpec((tile, PAIR), lambda j, i: (i, j))] + [both] * parts,
        out_shape=[jax.ShapeDtypeStruct((rows, count * PAIR), BF16)]
        + [jax.ShapeDtypeStruct((2, rows, count * PAIR), BF16)] * parts,
        scratch_shapes=[pltpu.VMEM((PAIR, keys), BF16)] + [all_keys] * 2 + [turned_keys] * 2,
        compiler_params=params(),
        cost_estimate=pl.CostEstimate(
            flops=32 * rows * keys * width // groups,
            bytes_accessed=4 * count * rows * keys,
            transcendentals=0,
        ),
        name="attend_back",
    )(q, inverse, att, datt, p, *kv_parts, *kv_parts, *after)
    return out[0], out[1:]


def gelu_parts(u):
    base = 1.0 + (0.3275911 * math.sqrt(0.5)) * jnp.abs(u)
    t = pl.reciprocal(base, approx=True)
    bell = jnp.exp2(u * u * (-0.5 * LOG2E))
    series = t * (
        0.5 * 0.254829592
        + t
        * (
            0.5 * -0.284496736
            + t * (0.5 * 1.421413741 + t * (0.5 * -1.453152027 + t * (0.5 * 1.061405429)))
        )
    )
    tail = series * bell
    share = jnp.where(u < 0.0, tail, 1.0 - tail)
    return u * share, share + u * bell * (1.0 / math.sqrt(2.0 * math.pi))


def pieces_of(rows, most):
    piece = min(most, rows)
    return [slice(at, at + piece) for at in range(0, rows, piece)]


def feed_kernel(x, tile, last, *refs):
    att_ref, wout_ref, gain_ref, bias_ref, wup_ref, wdown_ref = refs[x.count() : x.count() + 6]
    mid_ref, h_ref, att_turned_ref, act_ref, slope_ref = refs[x.count() + 6 : x.count() + 11]
    if last:
        own_ref, away_ref, h_kept, next_ref = refs[x.count() + 11 :]
    else:
        next_ref, h_kept = refs[x.count() + 11 :]

    @pl.when(pl.program_id(1) == 0)
    def _():
        middle = x.read(tile, refs[: x.count()]) + mm(att_ref[...], wout_ref[...])
        mid_ref[...] = middle
        next_ref[...] = middle
        att_turned_ref[...] = turned(att_ref[...].astype(F32))
        n, _ = normalise(middle)
        h = n * gain_ref[1:2, :] + bias_ref[1:2, :]
        h_ref[...] = turned(h)
        h_kept[...] = h.astype(BF16)

    pieces = pieces_of(tile, 256)
    ups = [mm(h_kept[pieces[0], :], wup_ref[...])]
    for i, piece in enumerate(pieces):
        if i + 1 < len(pieces):
            ups.append(mm(h_kept[pieces[i + 1], :], wup_ref[...]))
        active, slope = gelu_parts(ups[i])
        active = active.astype(BF16)
        act_ref[piece, :] = active
        slope_ref[piece, :] = slope.astype(BF16)
        next_ref[piece, :] += mm(active, wdown_ref[...])
    if last:
        ends = pl.program_id(1) == pl.num_programs(1) - 1
        own = pl.program_id(0) < pl.num_programs(0) // 2

        @pl.when(ends & own)
        def _():
            own_ref[...] = next_ref[...]

        @pl.when(ends & jnp.logical_not(own))
        def _():
            away_ref[...] = next_ref[...].astype(BF16)


def across(spec):
    return pl.BlockSpec(
        spec.block_shape, lambda i, c: spec.index_map(i), pipeline_mode=spec.pipeline_mode
    )


def feed_weights(layer, width, chunk):
    up = pl.BlockSpec((None, width, chunk), lambda i, c: (layer, 0, c))
    down = pl.BlockSpec((None, chunk, width), lambda i, c: (layer, c, 0))
    return up, down


def feed_forward(layer, last, att, x, wout, gain, bias, wup, wdown):
    rows, width = x.rows, x.width
    hidden = wup.shape[2]
    tile = min(512, rows // 2)
    chunk = 512
    wide = pl.BlockSpec((tile, chunk), lambda i, c: (i, c))
    tiles = rows // 2 // tile
    halves = [
        pl.BlockSpec((tile, width), lambda i, c: (jnp.minimum(i, tiles - 1), 0)),
        pl.BlockSpec((tile, width), lambda i, c: (jnp.maximum(i - tiles, 0), 0)),
    ]
    return pl.pallas_call(
        functools.partial(feed_kernel, x, tile, last),
        grid=(rows // tile, hidden // chunk),
        in_specs=[
            across(spec)
            for spec in x.specs(tile)
            + [rows_of(tile, width)]
            + [layer_of(value, layer) for value in (wout, gain, bias)]
        ]
        + list(feed_weights(layer, width, chunk)),
        out_specs=[
            across(rows_of(tile, width)),
            across(columns_of(width, tile)),
            across(columns_of(width, tile)),
            wide,
            wide,
        ]
        + (halves if last else [across(rows_of(tile, width))]),
        out_shape=[
            jax.ShapeDtypeStruct((rows, width), F32),
            jax.ShapeDtypeStruct((width, rows), BF16),
            jax.ShapeDtypeStruct((width, rows), BF16),
            jax.ShapeDtypeStruct((rows, hidden), BF16),
            jax.ShapeDtypeStruct((rows, hidden), BF16),
        ]
        + (
            [
                jax.ShapeDtypeStruct((rows // 2, width), F32),
                jax.ShapeDtypeStruct((rows // 2, width), BF16),
            ]
            if last
            else [jax.ShapeDtypeStruct((rows, width), F32)]
        ),
        scratch_shapes=[pltpu.VMEM((tile, width), BF16)]
        + ([pltpu.VMEM((tile, width), F32)] if last else []),
        compiler_params=params(),
        cost_estimate=pl.CostEstimate(
            flops=2 * rows * width * (width + 2 * hidden),
            bytes_accessed=16 * rows * width + 4 * rows * hidden + 4 * width * hidden,
            transcendentals=2 * rows * hidden,
        ),
        name="feed",
    )(*x.operands(), att, wout, gain, bias, wup, wdown)


def add_norm_sums(first_row, sum_ref, e, n):
    bias_row = first_row + 2 * LAYERS
    sum_ref[first_row : first_row + 1, :] += jnp.sum(e * n, axis=0, keepdims=True)
    sum_ref[bias_row : bias_row + 1, :] += jnp.sum(e, axis=0, keepdims=True)


def feed_back_kernel(layer, grad, dp_size, core_ref, *refs):
    count = grad.count()
    (
        slope_ref,
        act_ref,
        mid_ref,
        h_ref,
        att_ref,
        gain_ref,
        wup_ref,
        wdown_ref,
        wout_ref,
        start_ref,
        up_gone,
        up_kept,
        down_gone,
        down_kept,
        dmid_ref,
        datt_ref,
        sum_ref,
        gy_ref,
        gy_turned_ref,
        total_ref,
    ) = refs[count:]
    core = core_ref[0]
    step = pl.program_id(0)
    rows, width = gy_ref.shape
    chunk = slope_ref.shape[1]
    half = up_gone.shape[1]
    slabs = 2 * half
    deep = width // dp_size
    thin = width // slabs
    wide = up_gone.shape[3] - thin

    @pl.when(step == 0)
    def _():
        value = grad.read(rows, refs[:count])
        gy_ref[...] = value.astype(BF16)
        gy_turned = turned(value)
        for s in range(slabs):
            at = s // 2 * thin
            gy_turned_ref[s % 2, at : at + thin, :] = gy_turned[s * thin : (s + 1) * thin, :]
        total_ref[...] = jnp.zeros_like(total_ref)

    pieces = pieces_of(rows, 512)
    dups = []
    for piece in pieces:
        inner = mm_nt(gy_ref[piece, :], wdown_ref[...])
        dups.append((inner * slope_ref[piece, :].astype(F32)).astype(BF16))
    dup = dups[0] if len(dups) == 1 else jnp.concatenate(dups, axis=0)
    for piece, one in zip(pieces, dups):
        total_ref[piece, :] += mm_nt(one, wup_ref[...])
    for k in range(chunk // wide):
        slab = step * (chunk // wide) + k
        product = mm(h_ref[...], dup[:, k * wide : (k + 1) * wide]).astype(BF16)
        for goes, out_ref in ((slab % 2 != core, up_gone), (slab % 2 == core, up_kept)):

            @pl.when(goes)
            def _(product=product, out_ref=out_ref, slab=slab):
                for d in range(dp_size):
                    out_ref[d, slab // 2, :, :wide] = product[d * deep : (d + 1) * deep, :]

    active = act_ref[...]
    pair, _, _, across_wide = down_gone.shape
    for which, out_ref in ((1 - core, down_gone), (core, down_kept)):
        product = mm(gy_turned_ref[which], active).astype(BF16)
        for x in range(half):
            for d in range(pair):
                out_ref[d, x] = product[
                    x * thin : (x + 1) * thin, d * across_wide : (d + 1) * across_wide
                ]

    @pl.when(step == pl.num_programs(0) - 1)
    def _():
        total = total_ref[...]
        n, r = normalise(mid_ref[...])
        dmid = grad.read(rows, refs[:count]) + norm_backward(n, r, total, gain_ref[1:2, :])
        dmid_ref[...] = dmid
        gz = dmid.astype(BF16)
        datt_ref[...] = mm_nt(gz, wout_ref[...]).astype(BF16)
        sum_ref[...] = start_ref[...]
        add_norm_sums(2 * layer + 1, sum_ref, total, n)
        product = mm(att_ref[...], gz).astype(BF16)
        for own in range(2):

            @pl.when(core == own)
            def _(own=own):
                for s in range(slabs):
                    out_ref = up_kept if s % 2 == own else up_gone
                    for d in range(dp_size):
                        out_ref[d, s // 2, :, wide:] = product[
                            d * deep : (d + 1) * deep, s * thin : (s + 1) * thin
                        ]


def feed_backward(
    layer,
    grad,
    slope,
    active,
    mid,
    h,
    att_turned,
    gain,
    wdown,
    wup,
    wout,
    start,
    core,
    slabs,
    dp_size,
    after,
):
    rows, width = grad.rows, grad.width
    hidden = wup.shape[2]
    half = slabs // 2
    wide, thin = hidden // slabs, width // slabs
    chunk = max(wide, 768)
    down_wide = hidden // dp_size
    pair = chunk // down_wide

    def fixed(shape):
        return pl.BlockSpec(
            shape, lambda c, core: (0,) * len(shape), pipeline_mode=pl.Buffered(1)
        )

    def of_layer(stacked):
        rest = stacked.shape[1:]
        return pl.BlockSpec(
            (None,) + rest,
            lambda c, core: (layer,) + (0,) * len(rest),
            pipeline_mode=pl.Buffered(1),
        )

    by_chunk = pl.BlockSpec((rows, chunk), lambda c, core: (0, c))
    up_shape = (dp_size, half, width // dp_size, wide + thin)
    down_shape = (dp_size, half, thin, down_wide)
    down_spec = pl.BlockSpec((pair, half, thin, down_wide), lambda c, core: (c, 0, 0, 0))
    return pl.pallas_call(
        without(
            functools.partial(feed_back_kernel, layer, grad, dp_size),
            1 + grad.count() + 10,
            len(after),
        ),
        grid_spec=pltpu.PrefetchScalarGridSpec(
            num_scalar_prefetch=1,
            grid=(hidden // chunk,),
            in_specs=[fixed(operand.shape) for operand in grad.operands()]
            + [by_chunk, by_chunk]
            + [fixed(one.shape) for one in (mid, h, att_turned)]
            + [
                of_layer(gain),
                pl.BlockSpec((None, width, chunk), lambda c, core: (layer, 0, c)),
                pl.BlockSpec((None, chunk, width), lambda c, core: (layer, c, 0)),
                of_layer(wout),
                fixed(start.shape),
            ]
            + ordered(after),
            out_specs=[fixed(up_shape)] * 2
            + [down_spec] * 2
            + [fixed((rows, width))] * 2
            + [fixed(start.shape)],
            scratch_shapes=[
                pltpu.VMEM((rows, width), BF16),
                pltpu.VMEM((2, width // 2, rows), BF16),
                pltpu.VMEM((rows, width), F32),
            ],
        ),
        out_shape=[jax.ShapeDtypeStruct(up_shape, BF16)] * 2
        + [jax.ShapeDtypeStruct(down_shape, BF16)] * 2
        + [
            jax.ShapeDtypeStruct((rows, width), F32),
            jax.ShapeDtypeStruct((rows, width), BF16),
            jax.ShapeDtypeStruct(start.shape, F32),
        ],
        compiler_params=params(),
        cost_estimate=pl.CostEstimate(
            flops=4 * rows * width * (width + 2 * hidden),
            bytes_accessed=20 * rows * width + 4 * rows * hidden + 8 * width * hidden,
            transcendentals=0,
        ),
        name="feed_back",
    )(
        core,
        *grad.operands(),
        slope,
        active,
        mid,
        h,
        att_turned,
        gain,
        wup,
        wdown,
        wout,
        start,
        *after,
    )


def summed(refs):
    total = refs[0][...].astype(F32)
    for ref in refs[1:]:
        total += ref[...].astype(F32)
    return total.astype(BF16)


def joined(groups, parts, refs):
    dkv = [summed(refs[groups + g * parts : groups + (g + 1) * parts]) for g in range(groups)]
    pieces = [ref[...] for ref in refs[:groups]]
    pieces += [block[0] for block in dkv]
    pieces += [block[1] for block in dkv]
    return jnp.concatenate(pieces, axis=1)


def joined_specs(groups, parts, tile, width, offset=0):
    one = pl.BlockSpec((tile, width // groups), lambda i: (i + offset, 0))
    pair = pl.BlockSpec((2, tile, width // groups), lambda i: (0, i + offset, 0))
    return [one] * groups + [pair] * (groups * parts)


def qkv_grad_kernel(layer, groups, parts, x, tile, ends, core_ref, *refs):
    before = groups * (1 + parts)
    x_refs = refs[before : before + x.count()]
    gain_ref, w_ref, h_ref, dmid_ref, start_ref, species_ref = refs[before + x.count() :][:6]
    gone_ref, kept_ref, grad_ref, sum_ref, full_ref = refs[before + x.count() + 6 :]
    dp_size, half, deep, wide = gone_ref.shape
    step, steps = pl.program_id(0), pl.num_programs(0)
    full = joined(groups, parts, refs)
    full_ref[pl.ds(pl.multiple_of(step * tile, tile), tile), :] = full

    @pl.when(step == 0)
    def _():
        sum_ref[...] = start_ref[...]

    @pl.when(step < ends)
    def _():
        e = mm_nt(full, w_ref[...])
        n, r = normalise(x.read(tile, x_refs))
        grad = dmid_ref[...] + norm_backward(n, r, e, gain_ref[0:1, :])
        grad_ref[...] = grad.astype(grad_ref.dtype)
        add_norm_sums(2 * layer, sum_ref, e, n)
        if layer == 0:
            row = pl.ds(4 * LAYERS + species_ref[0], 1)
            sum_ref[row, :] += jnp.sum(grad, axis=0, keepdims=True)

    @pl.when(step == steps - 1)
    def _():
        first = h_ref.shape[1] // 2
        h = jnp.concatenate([h_ref[:, first:], h_ref[:, :first]], axis=1)
        for s in range(2 * half):
            product = mm(h, full_ref[:, s * wide : (s + 1) * wide]).astype(BF16)
            for own in range(2):

                @pl.when(core_ref[0] == own)
                def _(own=own, s=s, product=product):
                    out_ref = kept_ref if s % 2 == own else gone_ref
                    for d in range(dp_size):
                        out_ref[d, s // 2] = product[d * deep : (d + 1) * deep, :]


def qkv_gradients(
    layer, ends, kind, dq, dkv, x, gain, w, h, dmid, start, species, core, slabs, dp_size, after
):
    groups, parts = len(dq), len(dkv[0])
    rows, width = dmid.shape
    tile = min(256, rows // 2)
    tiles = rows // tile
    turn_to = tiles // 2
    half = slabs // 2
    shape = (dp_size, half, width // dp_size, 3 * width // slabs)

    def fixed(shape):
        return pl.BlockSpec(
            shape, lambda i, core: (0,) * len(shape), pipeline_mode=pl.Buffered(1)
        )

    def of_layer(stacked):
        rest = stacked.shape[1:]
        return pl.BlockSpec(
            (None,) + rest,
            lambda i, core: (layer,) + (0,) * len(rest),
            pipeline_mode=pl.Buffered(1),
        )

    def at(i):
        return lax.rem(i + turn_to, tiles)

    def used(i):
        return at(jnp.minimum(i, ends - 1))

    def out_at(i):
        return used(i) if ends == tiles else jnp.minimum(i, ends - 1)

    one = pl.BlockSpec((tile, width // groups), lambda i, core: (at(i), 0))
    both = pl.BlockSpec((2, tile, width // groups), lambda i, core: (0, at(i), 0))
    if ends == tiles:
        x_specs = [pl.BlockSpec((tile, width), lambda i, core: (used(i), 0))]
    else:
        x_specs = [pl.BlockSpec((tile, width), lambda i, core: (out_at(i), 0))]
    if x.shift is not None:
        x_specs.append(fixed((1, width)))
    return pl.pallas_call(
        without(
            functools.partial(qkv_grad_kernel, layer, groups, parts, x, tile, ends),
            1 + groups * (1 + parts) + x.count() + 6,
            len(after),
        ),
        grid_spec=pltpu.PrefetchScalarGridSpec(
            num_scalar_prefetch=1,
            grid=(tiles,),
            in_specs=[one] * groups
            + [both] * (groups * parts)
            + x_specs
            + [of_layer(gain), of_layer(w), fixed(h.shape)]
            + [pl.BlockSpec((tile, width), lambda i, core: (used(i), 0)), fixed(start.shape)]
            + [pl.BlockSpec(memory_space=pltpu.SMEM)]
            + ordered(after),
            out_specs=[fixed(shape)] * 2
            + [pl.BlockSpec((tile, width), lambda i, core: (out_at(i), 0)), fixed(start.shape)],
            scratch_shapes=[pltpu.VMEM((rows, 3 * width), BF16)],
        ),
        out_shape=[jax.ShapeDtypeStruct(shape, BF16)] * 2
        + [
            jax.ShapeDtypeStruct((ends * tile, width), kind),
            jax.ShapeDtypeStruct(start.shape, F32),
        ],
        compiler_params=params(),
        cost_estimate=pl.CostEstimate(
            flops=12 * rows * width * width, bytes_accessed=32 * rows * width, transcendentals=0
        ),
        name="qkv_grad",
    )(
        core,
        *dq,
        *[block for group in dkv for block in group],
        *x.operands(),
        gain,
        w,
        h,
        dmid,
        start,
        species,
        *after,
    )


def qkv_back_kernel(layer, groups, parts, x, tile, *refs):
    before = groups * (1 + parts)
    gain_ref, w_ref, dmid_ref, start_ref, species_ref = refs[before + x.count() :][:5]
    grad_ref, sum_ref = refs[before + x.count() + 5 :]
    full = joined(groups, parts, refs)
    e = mm_nt(full, w_ref[...])
    n, r = normalise(x.read(tile, refs[before : before + x.count()]))
    grad = dmid_ref[...] + norm_backward(n, r, e, gain_ref[0:1, :])
    grad_ref[...] = grad.astype(grad_ref.dtype)

    @pl.when(pl.program_id(0) == 0)
    def _():
        sum_ref[...] = start_ref[...]

    add_norm_sums(2 * layer, sum_ref, e, n)
    if layer == 0:
        row = pl.ds(4 * LAYERS + species_ref[0], 1)
        sum_ref[row, :] += jnp.sum(grad, axis=0, keepdims=True)


def qkv_backward(layer, first_row, kind, dq, dkv, x, gain, w, dmid, start, species, after):
    groups, parts = len(dq), len(dkv[0])
    rows, width = x.rows, x.width
    tile = min(256, dmid.shape[0] // 2)
    offset = first_row // tile
    sums = pl.BlockSpec(start.shape, lambda i: (0, 0))
    return pl.pallas_call(
        without(
            functools.partial(qkv_back_kernel, layer, groups, parts, x, tile),
            groups * (1 + parts) + x.count() + 5,
            len(after),
        ),
        grid=(rows // tile,),
        in_specs=joined_specs(groups, parts, tile, width, offset)
        + x.specs(tile)
        + [layer_of(gain, layer), layer_of(w, layer)]
        + [pl.BlockSpec((tile, width), lambda i: (i + offset, 0)), sums]
        + [pl.BlockSpec(memory_space=pltpu.SMEM)]
        + ordered(after),
        out_specs=[rows_of(tile, width), sums],
        out_shape=[
            jax.ShapeDtypeStruct((rows, width), kind),
            jax.ShapeDtypeStruct(start.shape, F32),
        ],
        compiler_params=params(),
        cost_estimate=pl.CostEstimate(
            flops=6 * rows * width * width, bytes_accessed=24 * rows * width, transcendentals=0
        ),
        name="qkv_back",
    )(
        *dq,
        *[block for group in dkv for block in group],
        *x.operands(),
        gain,
        w,
        dmid,
        start,
        species,
        *after,
    )


def token_of(ref):
    ref[...] = jnp.zeros_like(ref)


TOKEN = jax.ShapeDtypeStruct((8, 128), F32)


def place_kernel(mine_ref, own_ref, came_ref, out_ref, token_ref):
    token_of(token_ref)
    mine = pl.program_id(0) == mine_ref[0]
    out_ref[...] = jnp.where(mine, own_ref[...], came_ref[...].astype(F32))


def place_cells(mine, value, came):
    rows, width = came.shape
    tile = min(256, rows)
    spec = pl.BlockSpec((tile, width), lambda c, i, mine: (i, 0))
    return pl.pallas_call(
        place_kernel,
        grid_spec=pltpu.PrefetchScalarGridSpec(
            num_scalar_prefetch=1,
            grid=(2, rows // tile),
            in_specs=[spec, spec],
            out_specs=[
                pl.BlockSpec((None, tile, width), lambda c, i, mine: (c, i, 0)),
                pl.BlockSpec(TOKEN.shape, lambda c, i, mine: (0, 0)),
            ],
        ),
        out_shape=[jax.ShapeDtypeStruct((2, rows, width), F32), TOKEN],
        compiler_params=params(16),
        cost_estimate=pl.CostEstimate(
            flops=rows * width, bytes_accessed=20 * rows * width, transcendentals=0
        ),
        name="place_cells",
    )(mine, value, came)


class Sum:
    def __init__(self, came, kept, steps, sizes, places, layer, results, scatter, part=(0, 1)):
        self.part = part
        self.whole = True
        self.sizes = sizes
        self.places = places
        self.scatter = scatter
        self.left = {
            "blk": bits_of(sizes["blk"])[1:],
            "dp": bits_of(sizes["dp"]),
        }
        self.steps = [step for step in steps if not scatter or step[0] == "blk"]
        self.layer = layer
        self.results = results
        self.kept = kept
        self.came = came
        self.over_blk = False
        self.waiting = 0
        self.finished = False

    def ready(self):
        ends = not (self.scatter or self.over_blk or self.steps)
        return not ends or self.layer == LAYERS - 1 or bool(self.results.held)

    def spread(self, call, outer, inner, tail):
        by_outer, by_inner = math.gcd(call.count, outer), math.gcd(call.count, inner)
        if by_outer >= by_inner:
            by = by_outer
            return (outer // by, 1, inner) + tail, lambda j, side: (
                j // (call.count // by),
                side,
                0,
                0,
                0,
            )
        by = by_inner
        return (outer, 1, inner // by) + tail, lambda j, side: (
            0,
            side,
            j // (call.count // by),
            0,
            0,
        )

    def prepare_scatter(self, call):
        tail = self.kept.shape[-2:]
        shape = (math.prod(self.kept.shape[:-2]), 1, 1) + tail
        block, index = self.spread(call, shape[0], 1, tail)
        spec = pl.BlockSpec(block, lambda j, side: index(j, 0))
        reads = [call.read(one.reshape(shape), spec) for one in (self.kept, self.came)]
        write = call.write(shape, BF16, spec)

        def work(refs):
            refs[write][...] = refs[reads[0]][...] + refs[reads[1]][...]

        def finish(out):
            whole = out(write).reshape((self.sizes["dp"], -1) + tail)
            self.kept = lax.psum_scatter(whole, "dp", scatter_dimension=0, tiled=False)
            self.came = None
            self.left = {"blk": [], "dp": []}
            self.steps = []
            self.waiting = self.scatter
            self.scatter = 0
            self.over_blk = True

        return work, finish

    def prepare_over_blk(self, call):
        at = call.carry(self.kept)

        def finish(out):
            blk = self.sizes["blk"]
            cores = [list(range(core, blk, 2)) for core in range(2)]
            self.kept = lax.psum_scatter(
                out(at), "blk", scatter_dimension=0, axis_index_groups=cores, tiled=False
            )
            self.over_blk = False
            self.waiting = 2

        return (lambda refs: None), finish

    def prepare(self, call):
        if self.scatter:
            return self.prepare_scatter(call)
        if self.over_blk:
            return self.prepare_over_blk(call)
        if not self.steps:
            return self.prepare_last(call)
        axis, bit = self.steps[0]
        at = self.left[axis].index(bit)
        inner = 1 << at
        if axis == "dp":
            inner <<= len(self.left["blk"])
        total = 1 << (len(self.left["blk"]) + len(self.left["dp"]))
        outer = total // (2 * inner)
        tail = self.kept.shape[-2:]
        shape = (outer, 2, inner) + tail
        piece = 0
        if self.whole:
            piece = self.part[0]
            tail = (tail[0] // self.part[1], tail[1])
        block, index = self.spread(call, outer, inner, tail)
        side = (self.places[axis] // bit) % 2
        sources = [self.kept.reshape(shape)]
        if self.came is not None:
            sources.append(self.came.reshape(shape))
        reads = []
        for value in (1 - side, side):
            at = call.scalar(value)
            spec = pl.BlockSpec(
                block, lambda j, side, at=at: index(j, side[at])[:3] + (piece, 0)
            )
            reads.append([call.read(one, spec) for one in sources])
        spec = pl.BlockSpec(block, lambda j, side: index(j, 0))
        writes = [call.write((outer, 1, inner) + tail, BF16, spec) for _ in range(2)]

        def work(refs):
            for some, write in zip(reads, writes):
                values = [refs[i][...] for i in some]
                refs[write][...] = values[0] if len(values) == 1 else values[0] + values[1]

        def finish(out):
            self.steps.pop(0)
            self.left[axis].remove(bit)
            self.whole = False
            self.kept = out(writes[1])
            self.came = exchange(out(writes[0]), axis, self.sizes[axis], bit)

        return work, finish

    def prepare_last(self, call):
        rows, wide = self.kept.shape[-2:]
        spec = pl.BlockSpec((rows, wide), lambda j, side: (0, 0))
        sources = [one for one in (self.kept, self.came) if one is not None]
        reads = [call.read(one.reshape(rows, wide), spec) for one in sources]
        writes = []
        first, count = self.part
        for name, columns in self.results.names:
            block = (rows * count, columns)
            spec = pl.BlockSpec((None,) + block, lambda j, side: (self.layer, 0, 0))
            if name not in call.shared:
                held = self.results.held.get(name)
                call.shared[name] = call.write((LAYERS,) + block, F32, spec, held)
            writes.append(call.shared[name])

        def work(refs):
            total = refs[reads[0]][...].astype(F32)
            if len(reads) == 2:
                total += refs[reads[1]][...].astype(F32)
            at = 0
            for write, (_, columns) in zip(writes, self.results.names):
                refs[write][first * rows : (first + 1) * rows, :] = total[:, at : at + columns]
                at += columns

        def finish(out):
            self.finished = True
            for write, (name, _) in zip(writes, self.results.names):
                self.results.held[name] = out(write)

        return work, finish


class Results:
    def __init__(self, names):
        self.names = names
        self.held = {}


class SmallSum:
    def __init__(self, value, sizes):
        self.value = value
        self.sizes = sizes
        self.steps = []
        for axis in ("blk", "dp"):
            bits = bits_of(sizes[axis])
            apart = len(bits) - 2 if axis == "dp" and len(bits) > 2 else len(bits)
            self.steps += [(axis, (bit,)) for bit in bits[:apart]]
            if apart < len(bits):
                first, second = bits[apart:]
                self.steps.append((axis, (first, second, first + second)))
        self.came = None
        self.waiting = 0
        self.finished = False
        self.send()

    def ready(self):
        return True

    def send(self):
        axis, masks = self.steps.pop(0)
        self.came = [exchange(self.value, axis, self.sizes[axis], mask) for mask in masks]

    def prepare(self, call):
        shape = self.value.shape
        spec = pl.BlockSpec(shape, lambda j, side: (0, 0))
        reads = [call.read(one, spec) for one in [self.value] + self.came]
        if self.steps:
            writes = [call.write(shape, F32, spec)]
        else:
            norms = (LAYERS, 2, shape[1])
            spec = pl.BlockSpec(norms, lambda j, side: (0, 0, 0))
            writes = [call.write(norms, F32, spec) for _ in range(2)]
            spec = pl.BlockSpec((2, shape[1]), lambda j, side: (0, 0))
            writes.append(call.write((2, shape[1]), F32, spec))
        last = not self.steps

        def work(refs):
            values = [refs[i][...] for i in reads]
            while len(values) > 1:
                values = [a + b for a, b in zip(values[::2], values[1::2])]
            if not last:
                refs[writes[0]][...] = values[0]
                return
            for which in range(2):
                for row in range(2 * LAYERS):
                    at = which * 2 * LAYERS + row
                    refs[writes[which]][row // 2, row % 2 : row % 2 + 1, :] = values[0][
                        at : at + 1, :
                    ]
            refs[writes[2]][...] = values[0][4 * LAYERS : 4 * LAYERS + 2, :]

        def finish(out):
            if last:
                self.value = [out(write) for write in writes]
                self.finished = True
            else:
                self.value = out(writes[0])
                self.send()

        return work, finish


class Call:
    def __init__(self):
        self.count = 2
        self.scalars, self.operands, self.in_specs = [], [], []
        self.out_specs, self.shapes, self.held = [], [], []
        self.shared = {}

    def scalar(self, value):
        self.scalars.append(value)
        return len(self.scalars) - 1

    def read(self, operand, spec):
        self.operands.append(operand)
        self.in_specs.append(spec)
        return ("in", len(self.operands) - 1)

    def write(self, shape, kind, spec, held=None):
        self.shapes.append(jax.ShapeDtypeStruct(shape, kind))
        self.out_specs.append(spec)
        self.held.append(held)
        return ("out", len(self.shapes) - 1)

    def carry(self, operand):
        spec = pl.BlockSpec(memory_space=pl.ANY)
        return self.write(operand.shape, operand.dtype, spec, operand)


def fold(moving, after, passed=(), at_end=False):
    call = Call()
    call.scalar(jnp.int32(0))
    tasks = []
    for one in moving:
        if one.waiting:
            one.waiting -= 1
        elif one.ready():
            tasks.append(one.prepare(call))
    if not tasks:
        return after[0], passed
    token = call.write(
        TOKEN.shape, TOKEN.dtype, pl.BlockSpec(TOKEN.shape, lambda j, side: (0, 0))
    )
    tasks.append((lambda refs: token_of(refs[token]), lambda out: None))
    spare = pl.BlockSpec(memory_space=pl.ANY)
    kept_back = [(i, one) for i, one in enumerate(call.held) if one is not None]
    for array in passed:
        kept_back.append((len(call.shapes), array))
        call.shapes.append(jax.ShapeDtypeStruct(array.shape, array.dtype))
        call.out_specs.append(spare)
    inputs = len(call.operands)
    unused = len(kept_back) + len(after)

    def kernel(side_ref, *refs):
        where = {}
        for i in range(inputs):
            where[("in", i)] = refs[i]
        for i in range(len(call.shapes)):
            where[("out", i)] = refs[inputs + unused + i]
        for work, _ in tasks:
            work(where)

    size = sum(math.prod(shape.shape) for shape in call.shapes)
    out = pl.pallas_call(
        kernel,
        grid_spec=pltpu.PrefetchScalarGridSpec(
            num_scalar_prefetch=1,
            grid=(call.count,),
            in_specs=call.in_specs + [spare] * unused,
            out_specs=call.out_specs,
        ),
        out_shape=call.shapes,
        input_output_aliases={1 + inputs + i: at for i, (at, _) in enumerate(kept_back)},
        compiler_params=params(16 if at_end else 64),
        cost_estimate=pl.CostEstimate(flops=size, bytes_accessed=6 * size, transcendentals=0),
        name="fold",
    )(
        jnp.stack(call.scalars).astype(jnp.int32),
        *call.operands,
        *[array for _, array in kept_back],
        *after,
    )
    for _, finish in tasks:
        finish(lambda write: out[write[1]])
    moving[:] = [one for one in moving if not one.finished]
    return out[token[1]], tuple(out[len(out) - len(passed) :])


def exchange(value, axis, size, bit):
    return lax.ppermute(value, axis, [(i, i ^ bit) for i in range(size)])


def bits_of(size):
    return [1 << i for i in range(size.bit_length() - 1)]


def shards(
    dp_size,
    blk_size,
    embedded,
    species_flag,
    gene_ids,
    species_table,
    norm_gain,
    norm_bias,
    w_qkv,
    w_out,
    w_up,
    w_down,
    out_cotangent,
):
    _, block_len, width = embedded.shape
    half = blk_size // 2
    place = lax.axis_index("blk")
    mine = place // half

    def swap(value):
        return exchange(value, "blk", blk_size, half)

    def own_and_other(pair):
        return tuple(
            lax.dynamic_index_in_dim(pair, which, 0, keepdims=False)
            for which in (mine, 1 - mine)
        )

    def collect(pair):
        own, other = own_and_other(pair)
        return own, swap(other)

    def turn(value, by):
        pairs = []
        for b in range(blk_size):
            base, j = b // half * half, b % half
            pairs.append((b, base + (j - by) % half))
        return lax.ppermute(value, "blk", pairs)

    def gather_parts(value):
        return [value] + [turn(value, by) for by in range(1, half)]

    ids = jnp.concatenate(collect(gene_ids))
    dead = jnp.where(ids != 0, 0.0, MASKED).astype(BF16)
    dead_parts = [
        jnp.broadcast_to(part[:, None], (part.shape[0], PAIR)) for part in gather_parts(dead)
    ]
    species, _ = own_and_other(species_flag)
    picked = jnp.where(species == 0, species_table[0], species_table[1])
    state = Tokens(collect(embedded), picked[None, :])
    cotangent = Tokens(collect(out_cotangent))

    kept = []
    for layer in range(LAYERS):
        first = tuple(dead_parts) if layer == 0 else ()
        h1, q, kv = qkv_forward(layer, state, norm_gain, norm_bias, w_qkv, first)
        kv_parts = gather_parts(kv)
        att, inverse, p = attend(q, kv_parts, dead_parts)
        last_one = layer == LAYERS - 1
        mid, h2, att_turned, active, slope, *after = feed_forward(
            layer, last_one, att, state, w_out, norm_gain, norm_bias, w_up, w_down
        )
        kept.append(
            (state, h1, q, kv_parts, att, inverse, p, mid, h2, att_turned, active, slope)
        )
        state = Tokens(after)
    came = swap(after[1])
    hidden_out, placed = place_cells(mine[None], after[0], came)

    sizes = {"blk": blk_size, "dp": dp_size}
    places = {"blk": place, "dp": lax.axis_index("dp")}
    core = place % 2
    over_blk = [("blk", bit) for bit in bits_of(blk_size)[1:]]
    over_dp = [("dp", bit) for bit in bits_of(dp_size)]
    core = core[None]

    def column_sums(pair, orders, layer, results, waits):
        gone, own = (value.reshape((half * dp_size,) + value.shape[-2:]) for value in pair)
        came = exchange(gone, "blk", blk_size, 1)
        scatter = waits if layer > 0 else 0
        if own.shape[1] % (16 * len(orders)):
            orders = orders[:1]
        return [
            Sum(came, own, order, sizes, places, layer, results, scatter, (i, len(orders)))
            for i, order in enumerate(orders)
        ]

    up_width = w_up.shape[2] // blk_size
    of_up_out = Results([("up", up_width), ("out", width // blk_size)])
    of_down = Results([("down", w_down.shape[1] // dp_size)])
    of_qkv = Results([("qkv", 3 * width // blk_size)])
    groups = 2
    grad = cotangent
    moving = []
    last = ()
    small = jnp.zeros((16, width), F32)
    species = species[None]
    for layer in reversed(range(LAYERS)):
        x, h1, q, kv_parts, att, inverse, p, mid, h2, att_turned, active, slope = kept[layer]
        up_gone, up_kept, down_gone, down_kept, dmid, datt, small = feed_backward(
            layer,
            grad,
            slope,
            active,
            mid,
            h2,
            att_turned,
            norm_gain,
            w_down,
            w_up,
            w_out,
            small,
            core,
            blk_size,
            dp_size,
            last,
        )
        last = (datt,)
        if moving:
            added, _ = fold(moving, last)
            last = (added,)
        moving += column_sums((up_gone, up_kept), [over_blk + over_dp], layer, of_up_out, 3)
        moving += column_sums((down_gone, down_kept), [over_dp + over_blk], layer, of_down, 3)
        arrived = (came,)
        dq, dkv = [], []
        for group in range(groups):
            one_dq, one_dkv = attend_back(
                group, groups, q, inverse, att, datt, p, kv_parts, last
            )
            others = tuple(one_dkv[1:])
            if group == groups - 1:
                added, others = fold(moving, (one_dq,) + arrived, others)
            else:
                added, _ = fold(moving, (one_dq,) + arrived)
            arrived = tuple(turn(value, half - 1 - by) for by, value in enumerate(others))
            last = (added,)
            dq.append(one_dq)
            dkv.append((one_dkv[0],) + arrived)
        if layer > 0:
            orders = [over_dp + over_blk]
        else:
            near, far = over_dp[:1], over_dp[1:]
            orders = [near + over_blk + far, far[:1] + near + over_blk + far[1:]]
        tiles = 2 * block_len // min(256, block_len)
        ends = tiles if layer > 0 else tiles // 2
        moved = x if layer > 0 else Tokens([x.arrays[1]], x.shift)
        gone, own, one_grad, small = qkv_gradients(
            layer,
            ends,
            F32 if layer > 0 else BF16,
            dq,
            dkv,
            moved,
            norm_gain,
            w_qkv,
            h1,
            dmid,
            small,
            species,
            core,
            blk_size,
            dp_size,
            last,
        )
        if layer == 0:
            added, (one_grad, gone) = fold(moving, (own,), (one_grad, gone))
            last = (added,)
        moving += column_sums((gone, own), orders, layer, of_qkv, 0)
        if layer > 0:
            last = (one_grad,)
            grad = Tokens([one_grad])
        else:
            came = swap(one_grad)
            own_x = Tokens([x.arrays[0]], x.shift)
            own_grad, small = qkv_backward(
                layer, 0, F32, dq, dkv, own_x, norm_gain, w_qkv, dmid, small, species, last
            )
            added, (small,) = fold(moving, (own_grad,), (small,))
            last = (added,)
    small = SmallSum(small, sizes)
    moving.append(small)
    embed_grad, embed_placed = place_cells(mine[None], own_grad, came)
    last += (placed, embed_placed)
    while moving:
        added, _ = fold(moving, last, (), True)
        last = (added,)

    gain_grad, bias_grad, species_grad = small.value
    return (
        hidden_out,
        embed_grad,
        species_grad,
        gain_grad,
        bias_grad,
        of_qkv.held["qkv"],
        of_up_out.held["out"],
        of_up_out.held["up"],
        of_down.held["down"].transpose(0, 2, 1),
    )


def solution(mesh):
    placed = (
        P("dp", "blk", None),
        P("dp"),
        P("dp", "blk"),
        P(),
        P(),
        P(),
        P(),
        P(),
        P(),
        P(),
        P("dp", "blk", None),
    )
    return jax.shard_map(
        functools.partial(shards, mesh.shape["dp"], mesh.shape["blk"]),
        mesh=mesh,
        in_specs=placed,
        out_specs=(
            P("dp", "blk", None),
            P("dp", "blk", None),
            P(),
            P(),
            P(),
            P(None, "dp", "blk"),
            P(None, "dp", "blk"),
            P(None, "dp", "blk"),
            P(None, "dp", "blk"),
        ),
        check_vma=False,
    )
```

```python
import functools
import math

import jax
import jax.numpy as jnp
from jax import lax
from jax.experimental import pallas as pl
from jax.experimental.pallas import tpu as pltpu
from jax.sharding import PartitionSpec as P

HEADS = 12
HEAD_DIM = 64
LAYERS = 2
PAIR = 2 * HEAD_DIM
EPS = 1e-05
LOG2E = 1.4426950408889634
LN2 = 0.6931471805599453
SCALE = 1.0 / math.sqrt(HEAD_DIM)
MASKED = -1e30
MIB = 1024 * 1024

F32 = jnp.float32
BF16 = jnp.bfloat16


def mm(left, right):
    return jnp.dot(left, right, preferred_element_type=F32)


def mm_nt(left, right):
    return lax.dot_general(left, right, (((1,), (1,)), ((), ())), preferred_element_type=F32)


def mm_tn(left, right):
    return lax.dot_general(left, right, (((0,), (0,)), ((), ())), preferred_element_type=F32)


def pieced(product, left, right, axis):
    wide = right.shape[axis]
    pieces = [
        product(
            left[...],
            right[:, at : min(at + 256, wide)]
            if axis == 1
            else right[at : min(at + 256, wide), :],
        )
        for at in range(0, wide, 256)
    ]
    return pieces[0] if len(pieces) == 1 else jnp.concatenate(pieces, axis=1)


def normalise(value):
    mean = jnp.mean(value, axis=-1, keepdims=True)
    centred = value - mean
    variance = jnp.mean(centred * centred, axis=-1, keepdims=True)
    r = lax.rsqrt(variance + EPS)
    return centred * r, r


def norm_backward(n, r, e, gain):
    eg = e * gain
    first = jnp.mean(eg, axis=-1, keepdims=True)
    second = jnp.mean(eg * n, axis=-1, keepdims=True)
    return r * (eg - first - n * second)


def params(mib=64):
    return pltpu.CompilerParams(vmem_limit_bytes=mib * MIB)


def whole(shape):
    return pl.BlockSpec(shape, lambda i: (0,) * len(shape), pipeline_mode=pl.Buffered(1))


def rows_of(tile, width):
    return pl.BlockSpec((tile, width), lambda i: (i, 0))


def slabs_of(count, tile, width):
    return pl.BlockSpec((count, tile, width), lambda i: (0, i, 0))


def columns_of(width, tile):
    return pl.BlockSpec((width, tile), lambda i: (0, i))


def layer_of(stacked, layer):
    rest = stacked.shape[1:]
    return pl.BlockSpec(
        (None,) + rest, lambda i: (layer,) + (0,) * len(rest), pipeline_mode=pl.Buffered(1)
    )


def ordered(after):
    return [pl.BlockSpec(memory_space=pl.ANY)] * len(after)


def without(kernel, first, count):
    def run(*refs):
        return kernel(*refs[:first], *refs[first + count :])

    return run


def turned(value):
    return value.T.astype(BF16)


def token_of(ref):
    ref[...] = jnp.zeros_like(ref)


TOKEN = jax.ShapeDtypeStruct((8, 128), F32)


class Tokens:
    def __init__(self, arrays, shift=None):
        self.arrays = arrays
        self.shift = shift
        self.rows = sum(array.shape[0] for array in arrays)
        self.width = arrays[0].shape[1]

    def operands(self):
        return list(self.arrays) + ([] if self.shift is None else [self.shift])

    def specs(self, tile):
        tiles = self.arrays[0].shape[0] // tile
        if len(self.arrays) == 1:
            specs = [rows_of(tile, self.width)]
        else:
            specs = [
                pl.BlockSpec((tile, self.width), lambda i: (jnp.minimum(i, tiles - 1), 0)),
                pl.BlockSpec((tile, self.width), lambda i: (jnp.maximum(i - tiles, 0), 0)),
            ]
        return specs + ([] if self.shift is None else [whole((1, self.width))])

    def count(self):
        return len(self.operands())

    def read(self, tile, refs):
        value = refs[0][...].astype(F32)
        if tile == self.rows and len(self.arrays) == 2:
            value = jnp.concatenate([value, refs[1][...].astype(F32)], axis=0)
        elif len(self.arrays) == 2:
            first = pl.program_id(0) < self.arrays[0].shape[0] // tile
            value = jnp.where(first, value, refs[1][...].astype(F32))
        return value if self.shift is None else value + refs[-1][...]


def qkv_kernel(x, tile, *refs):
    gain_ref, bias_ref, w_ref, h_ref, q_ref, kv_ref, token_ref = refs[x.count() :]
    token_of(token_ref)
    width = x.width
    n, _ = normalise(x.read(tile, refs[: x.count()]))
    h = n * gain_ref[0:1, :] + bias_ref[0:1, :]
    h_ref[...] = turned(h)
    h = h.astype(BF16)
    kv_ref[...] = mm(h, w_ref[:, width:]).astype(BF16)
    q_ref[...] = (mm(h, w_ref[:, :width]) * (SCALE * LOG2E)).astype(BF16)


def qkv_forward(layer, x, gain, bias, w, after, rows=None, held=None):
    width = x.width
    rows = rows or x.rows
    tile = min(256, rows // 2)
    held = held or []
    offset = (rows - x.rows) // tile if held else 0
    return pl.pallas_call(
        without(
            functools.partial(qkv_kernel, x, tile), x.count() + 3, len(held) + len(after)
        ),
        grid=(x.rows // tile,),
        in_specs=x.specs(tile)
        + [layer_of(value, layer) for value in (gain, bias, w)]
        + ordered(held)
        + ordered(after),
        out_specs=[
            pl.BlockSpec((width, tile), lambda i: (0, i + offset)),
            pl.BlockSpec((tile, width), lambda i: (i + offset, 0)),
            pl.BlockSpec((tile, 2 * width), lambda i: (i + offset, 0)),
            pl.BlockSpec(TOKEN.shape, lambda i: (0, 0)),
        ],
        out_shape=[
            jax.ShapeDtypeStruct((width, rows), BF16),
            jax.ShapeDtypeStruct((rows, width), BF16),
            jax.ShapeDtypeStruct((rows, 2 * width), BF16),
            TOKEN,
        ],
        input_output_aliases={x.count() + 3 + i: i for i in range(len(held))},
        compiler_params=params(),
        cost_estimate=pl.CostEstimate(
            flops=6 * x.rows * width * width,
            bytes_accessed=12 * x.rows * width,
            transcendentals=0,
        ),
        name="norm_qkv",
    )(*x.operands(), gain, bias, w, *held, *after)


def lanes_like(shape):
    lane = lax.broadcasted_iota(jnp.int32, shape, 1)
    return lane < HEAD_DIM, lane & (HEAD_DIM - 1)


def three_parts(value, sub, fourth):
    high = value.astype(BF16).astype(F32)
    rest = value - high
    middle = rest.astype(BF16).astype(F32)
    least = rest - middle
    return jnp.where(
        sub == 0,
        high,
        jnp.where(sub == 1, middle, jnp.where(sub == 2, least, jnp.where(sub == 3, fourth, 0.0))),
    )


def attend_kernel(parts, *refs):
    q_ref = refs[0]
    k_refs = refs[1 : 1 + parts]
    v_refs = refs[1 + parts : 1 + 2 * parts]
    dead_refs = refs[1 + 2 * parts : 1 + 3 * parts]
    o_ref, inverse_ref, p_ref, ka, kb, va, vb = refs[1 + 3 * parts :]
    rows = k_refs[0].shape[0]

    @pl.when(pl.program_id(1) == 0)
    def _():
        low, sub = lanes_like((rows, PAIR))
        for part in range(parts):
            own = slice(part * rows, (part + 1) * rows)
            k = k_refs[part][...].astype(F32)
            v = v_refs[part][...].astype(F32)
            extra = jnp.where(sub == 3, dead_refs[part][...].astype(F32), 0.0)
            ka[own, :] = jnp.where(low, k, extra).astype(BF16)
            kb[own, :] = jnp.where(low, extra, k).astype(BF16)
            va[own, :] = jnp.where(low, v, 1.0).astype(BF16)
            vb[own, :] = jnp.where(low, 1.0, v).astype(BF16)

    low, sub = lanes_like(q_ref.shape)
    fourth = jnp.where(sub == 3, 1.0, 0.0)
    q = q_ref[...].astype(F32)
    sa = mm_nt(jnp.where(low, q, fourth).astype(BF16), ka[...])
    sb = mm_nt(jnp.where(low, fourth, q).astype(BF16), kb[...])
    pa = jnp.exp2(sa - jnp.max(sa, axis=-1, keepdims=True)).astype(BF16)
    p_ref[0] = pa
    oa = mm(pa, va[...])
    pb = jnp.exp2(sb - jnp.max(sb, axis=-1, keepdims=True)).astype(BF16)
    p_ref[1] = pb
    ob = mm(pb, vb[...])
    inverse = 1.0 / pltpu.roll(jnp.where(low, ob, oa), HEAD_DIM, 1)
    inverse_ref[...] = inverse
    o_ref[...] = (jnp.where(low, oa, ob) * inverse).astype(BF16)


def attend(q, kv_parts, dead_parts):
    rows, width = q.shape
    parts = len(kv_parts)
    pairs = width // PAIR
    tile = min(512, rows)
    keys = parts * rows
    some = pl.BlockSpec((tile, PAIR), lambda j, i: (i, j))
    first = pl.BlockSpec((rows, PAIR), lambda j, i: (0, j))
    second = pl.BlockSpec((rows, PAIR), lambda j, i: (0, pairs + j))
    fixed = pl.BlockSpec((rows, PAIR), lambda j, i: (0, 0))
    scratch = pltpu.VMEM((keys, PAIR), BF16)
    return pl.pallas_call(
        functools.partial(attend_kernel, parts),
        grid=(pairs, rows // tile),
        in_specs=[some] + [first] * parts + [second] * parts + [fixed] * parts,
        out_specs=[some, some, pl.BlockSpec((2, tile, keys), lambda j, i: (j, i, 0))],
        out_shape=[
            jax.ShapeDtypeStruct((rows, width), BF16),
            jax.ShapeDtypeStruct((rows, width), F32),
            jax.ShapeDtypeStruct((2 * pairs, rows, keys), BF16),
        ],
        scratch_shapes=[scratch] * 4,
        compiler_params=params(),
        cost_estimate=pl.CostEstimate(
            flops=16 * rows * keys * width,
            bytes_accessed=4 * pairs * rows * keys,
            transcendentals=HEADS * rows * keys,
        ),
        name="attend",
    )(q, *kv_parts, *kv_parts, *dead_parts)


def attend_back_kernel(parts, *refs):
    q_ref, inverse_ref, att_ref, datt_ref, p_ref = refs[:5]
    k_refs = refs[5 : 5 + parts]
    v_refs = refs[5 + parts : 5 + 2 * parts]
    rest = refs[5 + 2 * parts :]
    dq_ref = rest[0]
    dkv_refs = rest[1 : 1 + parts]
    ks, va, vb, dk_turned, dv_turned = rest[1 + parts :]
    rows = k_refs[0].shape[0]
    index = pl.program_id(1)

    @pl.when(index == 0)
    def _():
        low, sub = lanes_like((rows, PAIR))
        ones = jnp.where(sub < 3, 1.0, 0.0)
        for part in range(parts):
            own = slice(part * rows, (part + 1) * rows)
            ks[own, :] = k_refs[part][...]
            v = v_refs[part][...].astype(F32)
            va[own, :] = jnp.where(low, v, ones).astype(BF16)
            vb[own, :] = jnp.where(low, ones, v).astype(BF16)
        dk_turned[...] = jnp.zeros_like(dk_turned)
        dv_turned[...] = jnp.zeros_like(dv_turned)

    low, sub = lanes_like(q_ref.shape)
    q_turned = turned(q_ref[...].astype(F32))
    datt = datt_ref[...].astype(F32) * inverse_ref[...]
    datt_turned = turned(datt)
    product = datt * att_ref[...].astype(F32)
    term_a = jnp.sum(jnp.where(low, product, 0.0), axis=-1, keepdims=True)
    term_b = jnp.sum(jnp.where(low, 0.0, product), axis=-1, keepdims=True)
    extra = three_parts(-jnp.where(low, term_b, term_a), sub, 0.0)
    ta = mm_nt(jnp.where(low, datt, extra).astype(BF16), va[...])
    tb = mm_nt(jnp.where(low, extra, datt).astype(BF16), vb[...])
    first, second = slice(0, HEAD_DIM), slice(HEAD_DIM, PAIR)
    pa, pb = p_ref[0], p_ref[1]
    dv_turned[first, :] += mm(datt_turned[first, :], pa)
    ga = (pa.astype(F32) * ta).astype(BF16)
    dqa = mm(ga, ks[...])
    dk_turned[first, :] += mm(q_turned[first, :], ga)
    dv_turned[second, :] += mm(datt_turned[second, :], pb)
    gb = (pb.astype(F32) * tb).astype(BF16)
    dqb = mm(gb, ks[...])
    dk_turned[second, :] += mm(q_turned[second, :], gb)
    dq_ref[...] = (jnp.where(low, dqa, dqb) * SCALE).astype(BF16)

    @pl.when(index == pl.num_programs(1) - 1)
    def _():
        for part in range(parts):
            own = slice(part * rows, (part + 1) * rows)
            dkv_refs[part][0] = (dk_turned[:, own].T * LN2).astype(BF16)
            dkv_refs[part][1] = dv_turned[:, own].T.astype(BF16)


def attend_back(group, groups, q, inverse, att, datt, p, kv_parts, after):
    rows, width = q.shape
    parts = len(kv_parts)
    pairs = width // PAIR
    count = pairs // groups
    base = group * count
    tile = min(512, rows)
    keys = parts * rows
    some = pl.BlockSpec((tile, PAIR), lambda j, i: (i, base + j))
    first = pl.BlockSpec((rows, PAIR), lambda j, i: (0, base + j))
    second = pl.BlockSpec((rows, PAIR), lambda j, i: (0, pairs + base + j))
    both = pl.BlockSpec((2, rows, PAIR), lambda j, i: (0, 0, j))
    all_keys = pltpu.VMEM((keys, PAIR), BF16)
    turned_keys = pltpu.VMEM((PAIR, keys), F32)
    out = pl.pallas_call(
        without(functools.partial(attend_back_kernel, parts), 5 + 2 * parts, len(after)),
        grid=(count, rows // tile),
        in_specs=[some] * 4
        + [pl.BlockSpec((2, tile, keys), lambda j, i: (base + j, i, 0))]
        + [first] * parts
        + [second] * parts
        + ordered(after),
        out_specs=[pl.BlockSpec((tile, PAIR), lambda j, i: (i, j))] + [both] * parts,
        out_shape=[jax.ShapeDtypeStruct((rows, count * PAIR), BF16)]
        + [jax.ShapeDtypeStruct((2, rows, count * PAIR), BF16)] * parts,
        scratch_shapes=[all_keys] * 3 + [turned_keys] * 2,
        compiler_params=params(),
        cost_estimate=pl.CostEstimate(
            flops=32 * rows * keys * width // groups,
            bytes_accessed=4 * count * rows * keys,
            transcendentals=0,
        ),
        name="attend_back",
    )(q, inverse, att, datt, p, *kv_parts, *kv_parts, *after)
    return out[0], out[1:]


def gelu_parts(u):
    base = 1.0 + (0.3275911 * math.sqrt(0.5)) * jnp.abs(u)
    t = pl.reciprocal(base, approx=True)
    bell = jnp.exp2(u * u * (-0.5 * LOG2E))
    series = t * (
        0.5 * 0.254829592
        + t
        * (
            0.5 * -0.284496736
            + t * (0.5 * 1.421413741 + t * (0.5 * -1.453152027 + t * (0.5 * 1.061405429)))
        )
    )
    tail = series * bell
    share = jnp.where(u < 0.0, tail, 1.0 - tail)
    return u * share, share + u * bell * (1.0 / math.sqrt(2.0 * math.pi))


def pieces_of(rows, most):
    piece = min(most, rows)
    return [slice(at, at + piece) for at in range(0, rows, piece)]


def feed_kernel(x, tile, last, *refs):
    att_ref, wout_ref, gain_ref, bias_ref, wup_ref, wdown_ref = refs[x.count() : x.count() + 6]
    mid_ref, h_ref, att_turned_ref, act_ref, slope_ref = refs[x.count() + 6 : x.count() + 11]
    if last:
        own_ref, away_ref, h_kept, next_ref = refs[x.count() + 11 :]
    else:
        next_ref, h_kept = refs[x.count() + 11 :]

    @pl.when(pl.program_id(1) == 0)
    def _():
        middle = x.read(tile, refs[: x.count()]) + mm(att_ref[...], wout_ref[...])
        mid_ref[...] = middle
        next_ref[...] = middle
        att_turned_ref[...] = turned(att_ref[...].astype(F32))
        n, _ = normalise(middle)
        h = n * gain_ref[1:2, :] + bias_ref[1:2, :]
        h_ref[...] = turned(h)
        h_kept[...] = h.astype(BF16)

    pieces = pieces_of(tile, 256)
    ups = [mm(h_kept[pieces[0], :], wup_ref[...])]
    for i, piece in enumerate(pieces):
        if i + 1 < len(pieces):
            ups.append(mm(h_kept[pieces[i + 1], :], wup_ref[...]))
        active, slope = gelu_parts(ups[i])
        active = active.astype(BF16)
        act_ref[piece, :] = active
        slope_ref[piece, :] = slope.astype(BF16)
        next_ref[piece, :] += mm(active, wdown_ref[...])
    if last:
        ends = pl.program_id(1) == pl.num_programs(1) - 1
        own = pl.program_id(0) < pl.num_programs(0) // 2

        @pl.when(ends & own)
        def _():
            own_ref[...] = next_ref[...]

        @pl.when(ends & jnp.logical_not(own))
        def _():
            away_ref[...] = next_ref[...].astype(BF16)


def across(spec):
    return pl.BlockSpec(
        spec.block_shape, lambda i, c: spec.index_map(i), pipeline_mode=spec.pipeline_mode
    )


def feed_weights(layer, width, chunk):
    up = pl.BlockSpec((None, width, chunk), lambda i, c: (layer, 0, c))
    down = pl.BlockSpec((None, chunk, width), lambda i, c: (layer, c, 0))
    return up, down


def feed_forward(layer, last, att, x, wout, gain, bias, wup, wdown):
    rows, width = x.rows, x.width
    hidden = wup.shape[2]
    tile = min(512, rows // 2)
    chunk = 512
    wide = pl.BlockSpec((tile, chunk), lambda i, c: (i, c))
    tiles = rows // 2 // tile
    halves = [
        pl.BlockSpec((tile, width), lambda i, c: (jnp.minimum(i, tiles - 1), 0)),
        pl.BlockSpec((tile, width), lambda i, c: (jnp.maximum(i - tiles, 0), 0)),
    ]
    return pl.pallas_call(
        functools.partial(feed_kernel, x, tile, last),
        grid=(rows // tile, hidden // chunk),
        in_specs=[
            across(spec)
            for spec in x.specs(tile)
            + [rows_of(tile, width)]
            + [layer_of(value, layer) for value in (wout, gain, bias)]
        ]
        + list(feed_weights(layer, width, chunk)),
        out_specs=[
            across(rows_of(tile, width)),
            across(columns_of(width, tile)),
            across(columns_of(width, tile)),
            wide,
            wide,
        ]
        + (halves if last else [across(rows_of(tile, width))]),
        out_shape=[
            jax.ShapeDtypeStruct((rows, width), F32),
            jax.ShapeDtypeStruct((width, rows), BF16),
            jax.ShapeDtypeStruct((width, rows), BF16),
            jax.ShapeDtypeStruct((rows, hidden), BF16),
            jax.ShapeDtypeStruct((rows, hidden), BF16),
        ]
        + (
            [
                jax.ShapeDtypeStruct((rows // 2, width), F32),
                jax.ShapeDtypeStruct((rows // 2, width), BF16),
            ]
            if last
            else [jax.ShapeDtypeStruct((rows, width), F32)]
        ),
        scratch_shapes=[pltpu.VMEM((tile, width), BF16)]
        + ([pltpu.VMEM((tile, width), F32)] if last else []),
        compiler_params=params(),
        cost_estimate=pl.CostEstimate(
            flops=2 * rows * width * (width + 2 * hidden),
            bytes_accessed=16 * rows * width + 4 * rows * hidden + 4 * width * hidden,
            transcendentals=2 * rows * hidden,
        ),
        name="feed",
    )(*x.operands(), att, wout, gain, bias, wup, wdown)


def add_norm_sums(first_row, sum_ref, e, n):
    bias_row = first_row + 2 * LAYERS
    sum_ref[first_row : first_row + 1, :] += jnp.sum(e * n, axis=0, keepdims=True)
    sum_ref[bias_row : bias_row + 1, :] += jnp.sum(e, axis=0, keepdims=True)


def feed_back_kernel(layer, grad, dp_size, core_ref, *refs):
    count = grad.count()
    (
        slope_ref,
        act_ref,
        mid_ref,
        h_ref,
        att_ref,
        gain_ref,
        wup_ref,
        wdown_ref,
        wout_ref,
        start_ref,
        up_gone,
        up_kept,
        down_gone,
        down_kept,
        dmid_ref,
        datt_ref,
        sum_ref,
        gy_ref,
        gy_turned_ref,
        total_ref,
    ) = refs[count:]
    core = core_ref[0]
    step = pl.program_id(0)
    rows, width = gy_ref.shape
    chunk = slope_ref.shape[1]
    half = up_gone.shape[1]
    slabs = 2 * half
    deep = width // dp_size
    thin = width // slabs
    wide = up_gone.shape[3] - thin

    @pl.when(step == 0)
    def _():
        value = grad.read(rows, refs[:count])
        gy_ref[...] = value.astype(BF16)
        gy_turned = turned(value)
        for s in range(slabs):
            at = s // 2 * thin
            gy_turned_ref[s % 2, at : at + thin, :] = gy_turned[s * thin : (s + 1) * thin, :]
        total_ref[...] = jnp.zeros_like(total_ref)

    pieces = pieces_of(rows, 512)
    dups = []
    for piece in pieces:
        inner = mm_nt(gy_ref[piece, :], wdown_ref[...])
        dups.append((inner * slope_ref[piece, :].astype(F32)).astype(BF16))
    dup = dups[0] if len(dups) == 1 else jnp.concatenate(dups, axis=0)
    for piece, one in zip(pieces, dups):
        total_ref[piece, :] += mm_nt(one, wup_ref[...])
    for k in range(chunk // wide):
        slab = step * (chunk // wide) + k
        product = mm(h_ref[...], dup[:, k * wide : (k + 1) * wide]).astype(BF16)
        for goes, out_ref in ((slab % 2 != core, up_gone), (slab % 2 == core, up_kept)):

            @pl.when(goes)
            def _(product=product, out_ref=out_ref, slab=slab):
                for d in range(dp_size):
                    out_ref[d, slab // 2, :, :wide] = product[d * deep : (d + 1) * deep, :]

    active = act_ref[...]
    pair, _, _, across_wide = down_gone.shape
    for which, out_ref in ((1 - core, down_gone), (core, down_kept)):
        product = mm(gy_turned_ref[which], active).astype(BF16)
        for x in range(half):
            for d in range(pair):
                out_ref[d, x] = product[
                    x * thin : (x + 1) * thin, d * across_wide : (d + 1) * across_wide
                ]

    @pl.when(step == pl.num_programs(0) - 1)
    def _():
        total = total_ref[...]
        n, r = normalise(mid_ref[...])
        dmid = grad.read(rows, refs[:count]) + norm_backward(n, r, total, gain_ref[1:2, :])
        dmid_ref[...] = dmid
        gz = dmid.astype(BF16)
        datt_ref[...] = mm_nt(gz, wout_ref[...]).astype(BF16)
        sum_ref[...] = start_ref[...]
        add_norm_sums(2 * layer + 1, sum_ref, total, n)
        product = mm(att_ref[...], gz).astype(BF16)
        for own in range(2):

            @pl.when(core == own)
            def _(own=own):
                for s in range(slabs):
                    out_ref = up_kept if s % 2 == own else up_gone
                    for d in range(dp_size):
                        out_ref[d, s // 2, :, wide:] = product[
                            d * deep : (d + 1) * deep, s * thin : (s + 1) * thin
                        ]


def feed_backward(
    layer,
    grad,
    slope,
    active,
    mid,
    h,
    att_turned,
    gain,
    wdown,
    wup,
    wout,
    start,
    core,
    slabs,
    dp_size,
    after,
):
    rows, width = grad.rows, grad.width
    hidden = wup.shape[2]
    half = slabs // 2
    wide, thin = hidden // slabs, width // slabs
    chunk = max(wide, 768)
    down_wide = hidden // dp_size
    pair = chunk // down_wide

    def fixed(shape):
        return pl.BlockSpec(
            shape, lambda c, core: (0,) * len(shape), pipeline_mode=pl.Buffered(1)
        )

    def of_layer(stacked):
        rest = stacked.shape[1:]
        return pl.BlockSpec(
            (None,) + rest,
            lambda c, core: (layer,) + (0,) * len(rest),
            pipeline_mode=pl.Buffered(1),
        )

    by_chunk = pl.BlockSpec((rows, chunk), lambda c, core: (0, c))
    up_shape = (dp_size, half, width // dp_size, wide + thin)
    down_shape = (dp_size, half, thin, down_wide)
    down_spec = pl.BlockSpec((pair, half, thin, down_wide), lambda c, core: (c, 0, 0, 0))
    return pl.pallas_call(
        without(
            functools.partial(feed_back_kernel, layer, grad, dp_size),
            1 + grad.count() + 10,
            len(after),
        ),
        grid_spec=pltpu.PrefetchScalarGridSpec(
            num_scalar_prefetch=1,
            grid=(hidden // chunk,),
            in_specs=[fixed(operand.shape) for operand in grad.operands()]
            + [by_chunk, by_chunk]
            + [fixed(one.shape) for one in (mid, h, att_turned)]
            + [
                of_layer(gain),
                pl.BlockSpec((None, width, chunk), lambda c, core: (layer, 0, c)),
                pl.BlockSpec((None, chunk, width), lambda c, core: (layer, c, 0)),
                of_layer(wout),
                fixed(start.shape),
            ]
            + ordered(after),
            out_specs=[fixed(up_shape)] * 2
            + [down_spec] * 2
            + [fixed((rows, width))] * 2
            + [fixed(start.shape)],
            scratch_shapes=[
                pltpu.VMEM((rows, width), BF16),
                pltpu.VMEM((2, width // 2, rows), BF16),
                pltpu.VMEM((rows, width), F32),
            ],
        ),
        out_shape=[jax.ShapeDtypeStruct(up_shape, BF16)] * 2
        + [jax.ShapeDtypeStruct(down_shape, BF16)] * 2
        + [
            jax.ShapeDtypeStruct((rows, width), F32),
            jax.ShapeDtypeStruct((rows, width), BF16),
            jax.ShapeDtypeStruct(start.shape, F32),
        ],
        compiler_params=params(),
        cost_estimate=pl.CostEstimate(
            flops=4 * rows * width * (width + 2 * hidden),
            bytes_accessed=20 * rows * width + 4 * rows * hidden + 8 * width * hidden,
            transcendentals=0,
        ),
        name="feed_back",
    )(
        core,
        *grad.operands(),
        slope,
        active,
        mid,
        h,
        att_turned,
        gain,
        wup,
        wdown,
        wout,
        start,
        *after,
    )


def summed(refs):
    total = refs[0][...].astype(F32)
    for ref in refs[1:]:
        total += ref[...].astype(F32)
    return total.astype(BF16)


def joined(groups, parts, refs):
    dkv = [summed(refs[groups + g * parts : groups + (g + 1) * parts]) for g in range(groups)]
    pieces = [ref[...] for ref in refs[:groups]]
    pieces += [block[0] for block in dkv]
    pieces += [block[1] for block in dkv]
    return jnp.concatenate(pieces, axis=1)


def joined_specs(groups, parts, tile, width, offset=0):
    one = pl.BlockSpec((tile, width // groups), lambda i: (i + offset, 0))
    pair = pl.BlockSpec((2, tile, width // groups), lambda i: (0, i + offset, 0))
    return [one] * groups + [pair] * (groups * parts)


def qkv_grad_kernel(layer, groups, parts, x, tile, ends, core_ref, *refs):
    before = groups * (1 + parts)
    x_refs = refs[before : before + x.count()]
    gain_ref, w_ref, h_ref, dmid_ref, start_ref, species_ref = refs[before + x.count() :][:6]
    gone_ref, kept_ref, grad_ref, sum_ref, full_ref = refs[before + x.count() + 6 :]
    dp_size, half, deep, wide = gone_ref.shape
    step, steps = pl.program_id(0), pl.num_programs(0)
    full = joined(groups, parts, refs)
    full_ref[pl.ds(pl.multiple_of(step * tile, tile), tile), :] = full

    @pl.when(step == 0)
    def _():
        sum_ref[...] = start_ref[...]

    @pl.when(step < ends)
    def _():
        e = mm_nt(full, w_ref[...])
        n, r = normalise(x.read(tile, x_refs))
        grad = dmid_ref[...] + norm_backward(n, r, e, gain_ref[0:1, :])
        grad_ref[...] = grad.astype(grad_ref.dtype)
        add_norm_sums(2 * layer, sum_ref, e, n)
        if layer == 0:
            row = pl.ds(4 * LAYERS + species_ref[0], 1)
            sum_ref[row, :] += jnp.sum(grad, axis=0, keepdims=True)

    @pl.when(step == steps - 1)
    def _():
        first = h_ref.shape[1] // 2
        h = jnp.concatenate([h_ref[:, first:], h_ref[:, :first]], axis=1)
        for s in range(2 * half):
            product = mm(h, full_ref[:, s * wide : (s + 1) * wide]).astype(BF16)
            for own in range(2):

                @pl.when(core_ref[0] == own)
                def _(own=own, s=s, product=product):
                    out_ref = kept_ref if s % 2 == own else gone_ref
                    for d in range(dp_size):
                        out_ref[d, s // 2] = product[d * deep : (d + 1) * deep, :]


def qkv_gradients(
    layer, ends, kind, dq, dkv, x, gain, w, h, dmid, start, species, core, slabs, dp_size, after
):
    groups, parts = len(dq), len(dkv[0])
    rows, width = dmid.shape
    tile = min(256, rows // 2)
    tiles = rows // tile
    turn_to = tiles // 2
    half = slabs // 2
    shape = (dp_size, half, width // dp_size, 3 * width // slabs)

    def fixed(shape):
        return pl.BlockSpec(
            shape, lambda i, core: (0,) * len(shape), pipeline_mode=pl.Buffered(1)
        )

    def of_layer(stacked):
        rest = stacked.shape[1:]
        return pl.BlockSpec(
            (None,) + rest,
            lambda i, core: (layer,) + (0,) * len(rest),
            pipeline_mode=pl.Buffered(1),
        )

    def at(i):
        return lax.rem(i + turn_to, tiles)

    def used(i):
        return at(jnp.minimum(i, ends - 1))

    def out_at(i):
        return used(i) if ends == tiles else jnp.minimum(i, ends - 1)

    one = pl.BlockSpec((tile, width // groups), lambda i, core: (at(i), 0))
    both = pl.BlockSpec((2, tile, width // groups), lambda i, core: (0, at(i), 0))
    if ends == tiles:
        x_specs = [pl.BlockSpec((tile, width), lambda i, core: (used(i), 0))]
    else:
        x_specs = [pl.BlockSpec((tile, width), lambda i, core: (out_at(i), 0))]
    if x.shift is not None:
        x_specs.append(fixed((1, width)))
    return pl.pallas_call(
        without(
            functools.partial(qkv_grad_kernel, layer, groups, parts, x, tile, ends),
            1 + groups * (1 + parts) + x.count() + 6,
            len(after),
        ),
        grid_spec=pltpu.PrefetchScalarGridSpec(
            num_scalar_prefetch=1,
            grid=(tiles,),
            in_specs=[one] * groups
            + [both] * (groups * parts)
            + x_specs
            + [of_layer(gain), of_layer(w), fixed(h.shape)]
            + [pl.BlockSpec((tile, width), lambda i, core: (used(i), 0)), fixed(start.shape)]
            + [pl.BlockSpec(memory_space=pltpu.SMEM)]
            + ordered(after),
            out_specs=[fixed(shape)] * 2
            + [pl.BlockSpec((tile, width), lambda i, core: (out_at(i), 0)), fixed(start.shape)],
            scratch_shapes=[pltpu.VMEM((rows, 3 * width), BF16)],
        ),
        out_shape=[jax.ShapeDtypeStruct(shape, BF16)] * 2
        + [
            jax.ShapeDtypeStruct((ends * tile, width), kind),
            jax.ShapeDtypeStruct(start.shape, F32),
        ],
        compiler_params=params(),
        cost_estimate=pl.CostEstimate(
            flops=12 * rows * width * width, bytes_accessed=32 * rows * width, transcendentals=0
        ),
        name="qkv_grad",
    )(
        core,
        *dq,
        *[block for group in dkv for block in group],
        *x.operands(),
        gain,
        w,
        h,
        dmid,
        start,
        species,
        *after,
    )


def qkv_back_kernel(layer, groups, parts, x, tile, *refs):
    before = groups * (1 + parts)
    gain_ref, w_ref, dmid_ref, start_ref, species_ref = refs[before + x.count() :][:5]
    grad_ref, sum_ref = refs[before + x.count() + 5 :]
    full = joined(groups, parts, refs)
    e = mm_nt(full, w_ref[...])
    n, r = normalise(x.read(tile, refs[before : before + x.count()]))
    grad = dmid_ref[...] + norm_backward(n, r, e, gain_ref[0:1, :])
    grad_ref[...] = grad.astype(grad_ref.dtype)

    @pl.when(pl.program_id(0) == 0)
    def _():
        sum_ref[...] = start_ref[...]

    add_norm_sums(2 * layer, sum_ref, e, n)
    if layer == 0:
        row = pl.ds(4 * LAYERS + species_ref[0], 1)
        sum_ref[row, :] += jnp.sum(grad, axis=0, keepdims=True)


def qkv_backward(layer, first_row, kind, dq, dkv, x, gain, w, dmid, start, species, after):
    groups, parts = len(dq), len(dkv[0])
    rows, width = x.rows, x.width
    tile = min(256, dmid.shape[0] // 2)
    offset = first_row // tile
    sums = pl.BlockSpec(start.shape, lambda i: (0, 0))
    return pl.pallas_call(
        without(
            functools.partial(qkv_back_kernel, layer, groups, parts, x, tile),
            groups * (1 + parts) + x.count() + 5,
            len(after),
        ),
        grid=(rows // tile,),
        in_specs=joined_specs(groups, parts, tile, width, offset)
        + x.specs(tile)
        + [layer_of(gain, layer), layer_of(w, layer)]
        + [pl.BlockSpec((tile, width), lambda i: (i + offset, 0)), sums]
        + [pl.BlockSpec(memory_space=pltpu.SMEM)]
        + ordered(after),
        out_specs=[rows_of(tile, width), sums],
        out_shape=[
            jax.ShapeDtypeStruct((rows, width), kind),
            jax.ShapeDtypeStruct(start.shape, F32),
        ],
        compiler_params=params(),
        cost_estimate=pl.CostEstimate(
            flops=6 * rows * width * width, bytes_accessed=24 * rows * width, transcendentals=0
        ),
        name="qkv_back",
    )(
        *dq,
        *[block for group in dkv for block in group],
        *x.operands(),
        gain,
        w,
        dmid,
        start,
        species,
        *after,
    )


def place_kernel(mine_ref, own_ref, came_ref, out_ref, token_ref):
    token_of(token_ref)
    mine = pl.program_id(0) == mine_ref[0]
    out_ref[...] = jnp.where(mine, own_ref[...], came_ref[...].astype(F32))


def place_cells(mine, value, came):
    rows, width = came.shape
    tile = min(256, rows)
    spec = pl.BlockSpec((tile, width), lambda c, i, mine: (i, 0))
    return pl.pallas_call(
        place_kernel,
        grid_spec=pltpu.PrefetchScalarGridSpec(
            num_scalar_prefetch=1,
            grid=(2, rows // tile),
            in_specs=[spec, spec],
            out_specs=[
                pl.BlockSpec((None, tile, width), lambda c, i, mine: (c, i, 0)),
                pl.BlockSpec(TOKEN.shape, lambda c, i, mine: (0, 0)),
            ],
        ),
        out_shape=[jax.ShapeDtypeStruct((2, rows, width), F32), TOKEN],
        compiler_params=params(16),
        cost_estimate=pl.CostEstimate(
            flops=rows * width, bytes_accessed=20 * rows * width, transcendentals=0
        ),
        name="place_cells",
    )(mine, value, came)


class Sum:
    def __init__(self, came, kept, steps, sizes, places, layer, results, scatter, part=(0, 1)):
        self.part = part
        self.whole = True
        self.sizes = sizes
        self.places = places
        self.scatter = scatter
        self.left = {
            "blk": bits_of(sizes["blk"])[1:],
            "dp": bits_of(sizes["dp"]),
        }
        self.steps = [step for step in steps if not scatter or step[0] == "blk"]
        self.layer = layer
        self.results = results
        self.kept = kept
        self.came = came
        self.over_blk = False
        self.waiting = 0
        self.finished = False

    def ready(self):
        ends = not (self.scatter or self.over_blk or self.steps)
        return not ends or self.layer == LAYERS - 1 or bool(self.results.held)

    def spread(self, call, outer, inner, tail):
        by_outer, by_inner = math.gcd(call.count, outer), math.gcd(call.count, inner)
        if by_outer >= by_inner:
            by = by_outer
            return (outer // by, 1, inner) + tail, lambda j, side: (
                j // (call.count // by),
                side,
                0,
                0,
                0,
            )
        by = by_inner
        return (outer, 1, inner // by) + tail, lambda j, side: (
            0,
            side,
            j // (call.count // by),
            0,
            0,
        )

    def prepare_scatter(self, call):
        tail = self.kept.shape[-2:]
        shape = (math.prod(self.kept.shape[:-2]), 1, 1) + tail
        block, index = self.spread(call, shape[0], 1, tail)
        spec = pl.BlockSpec(block, lambda j, side: index(j, 0))
        reads = [call.read(one.reshape(shape), spec) for one in (self.kept, self.came)]
        write = call.write(shape, BF16, spec)

        def work(refs):
            refs[write][...] = refs[reads[0]][...] + refs[reads[1]][...]

        def finish(out):
            whole = out(write).reshape((self.sizes["dp"], -1) + tail)
            self.kept = lax.psum_scatter(whole, "dp", scatter_dimension=0, tiled=False)
            self.came = None
            self.left = {"blk": [], "dp": []}
            self.steps = []
            self.waiting = self.scatter
            self.scatter = 0
            self.over_blk = True

        return work, finish

    def prepare_over_blk(self, call):
        at = call.carry(self.kept)

        def finish(out):
            blk = self.sizes["blk"]
            cores = [list(range(core, blk, 2)) for core in range(2)]
            self.kept = lax.psum_scatter(
                out(at), "blk", scatter_dimension=0, axis_index_groups=cores, tiled=False
            )
            self.over_blk = False
            self.waiting = 2

        return (lambda refs: None), finish

    def prepare(self, call):
        if self.scatter:
            return self.prepare_scatter(call)
        if self.over_blk:
            return self.prepare_over_blk(call)
        if not self.steps:
            return self.prepare_last(call)
        axis, bit = self.steps[0]
        at = self.left[axis].index(bit)
        inner = 1 << at
        if axis == "dp":
            inner <<= len(self.left["blk"])
        total = 1 << (len(self.left["blk"]) + len(self.left["dp"]))
        outer = total // (2 * inner)
        tail = self.kept.shape[-2:]
        shape = (outer, 2, inner) + tail
        piece = 0
        if self.whole:
            piece = self.part[0]
            tail = (tail[0] // self.part[1], tail[1])
        block, index = self.spread(call, outer, inner, tail)
        side = (self.places[axis] // bit) % 2
        sources = [self.kept.reshape(shape)]
        if self.came is not None:
            sources.append(self.came.reshape(shape))
        reads = []
        for value in (1 - side, side):
            at = call.scalar(value)
            spec = pl.BlockSpec(
                block, lambda j, side, at=at: index(j, side[at])[:3] + (piece, 0)
            )
            reads.append([call.read(one, spec) for one in sources])
        spec = pl.BlockSpec(block, lambda j, side: index(j, 0))
        writes = [call.write((outer, 1, inner) + tail, BF16, spec) for _ in range(2)]

        def work(refs):
            for some, write in zip(reads, writes):
                values = [refs[i][...] for i in some]
                refs[write][...] = values[0] if len(values) == 1 else values[0] + values[1]

        def finish(out):
            self.steps.pop(0)
            self.left[axis].remove(bit)
            self.whole = False
            self.kept = out(writes[1])
            self.came = exchange(out(writes[0]), axis, self.sizes[axis], bit)

        return work, finish

    def prepare_last(self, call):
        rows, wide = self.kept.shape[-2:]
        spec = pl.BlockSpec((rows, wide), lambda j, side: (0, 0))
        sources = [one for one in (self.kept, self.came) if one is not None]
        reads = [call.read(one.reshape(rows, wide), spec) for one in sources]
        writes = []
        first, count = self.part
        for name, columns in self.results.names:
            block = (rows * count, columns)
            spec = pl.BlockSpec((None,) + block, lambda j, side: (self.layer, 0, 0))
            if name not in call.shared:
                held = self.results.held.get(name)
                call.shared[name] = call.write((LAYERS,) + block, F32, spec, held)
            writes.append(call.shared[name])

        def work(refs):
            total = refs[reads[0]][...].astype(F32)
            if len(reads) == 2:
                total += refs[reads[1]][...].astype(F32)
            at = 0
            for write, (_, columns) in zip(writes, self.results.names):
                refs[write][first * rows : (first + 1) * rows, :] = total[:, at : at + columns]
                at += columns

        def finish(out):
            self.finished = True
            for write, (name, _) in zip(writes, self.results.names):
                self.results.held[name] = out(write)

        return work, finish


class Results:
    def __init__(self, names):
        self.names = names
        self.held = {}


class SmallSum:
    def __init__(self, value, sizes):
        self.value = value
        self.sizes = sizes
        self.steps = []
        for axis in ("blk", "dp"):
            bits = bits_of(sizes[axis])
            apart = len(bits) - 2 if axis == "dp" and len(bits) > 2 else len(bits)
            self.steps += [(axis, (bit,)) for bit in bits[:apart]]
            if apart < len(bits):
                first, second = bits[apart:]
                self.steps.append((axis, (first, second, first + second)))
        self.came = None
        self.waiting = 0
        self.finished = False
        self.send()

    def ready(self):
        return True

    def send(self):
        axis, masks = self.steps.pop(0)
        self.came = [exchange(self.value, axis, self.sizes[axis], mask) for mask in masks]

    def prepare(self, call):
        shape = self.value.shape
        spec = pl.BlockSpec(shape, lambda j, side: (0, 0))
        reads = [call.read(one, spec) for one in [self.value] + self.came]
        if self.steps:
            writes = [call.write(shape, F32, spec)]
        else:
            norms = (LAYERS, 2, shape[1])
            spec = pl.BlockSpec(norms, lambda j, side: (0, 0, 0))
            writes = [call.write(norms, F32, spec) for _ in range(2)]
            spec = pl.BlockSpec((2, shape[1]), lambda j, side: (0, 0))
            writes.append(call.write((2, shape[1]), F32, spec))
        last = not self.steps

        def work(refs):
            values = [refs[i][...] for i in reads]
            while len(values) > 1:
                values = [a + b for a, b in zip(values[::2], values[1::2])]
            if not last:
                refs[writes[0]][...] = values[0]
                return
            for which in range(2):
                for row in range(2 * LAYERS):
                    at = which * 2 * LAYERS + row
                    refs[writes[which]][row // 2, row % 2 : row % 2 + 1, :] = values[0][
                        at : at + 1, :
                    ]
            refs[writes[2]][...] = values[0][4 * LAYERS : 4 * LAYERS + 2, :]

        def finish(out):
            if last:
                self.value = [out(write) for write in writes]
                self.finished = True
            else:
                self.value = out(writes[0])
                self.send()

        return work, finish


class Call:
    def __init__(self):
        self.count = 2
        self.scalars, self.operands, self.in_specs = [], [], []
        self.out_specs, self.shapes, self.held = [], [], []
        self.shared = {}

    def scalar(self, value):
        self.scalars.append(value)
        return len(self.scalars) - 1

    def read(self, operand, spec):
        self.operands.append(operand)
        self.in_specs.append(spec)
        return ("in", len(self.operands) - 1)

    def write(self, shape, kind, spec, held=None):
        self.shapes.append(jax.ShapeDtypeStruct(shape, kind))
        self.out_specs.append(spec)
        self.held.append(held)
        return ("out", len(self.shapes) - 1)

    def carry(self, operand):
        spec = pl.BlockSpec(memory_space=pl.ANY)
        return self.write(operand.shape, operand.dtype, spec, operand)


def fold(moving, after, passed=(), at_end=False):
    call = Call()
    call.scalar(jnp.int32(0))
    tasks = []
    for one in moving:
        if one.waiting:
            one.waiting -= 1
        elif one.ready():
            tasks.append(one.prepare(call))
    if not tasks:
        return after[0], passed
    token = call.write(
        TOKEN.shape, TOKEN.dtype, pl.BlockSpec(TOKEN.shape, lambda j, side: (0, 0))
    )
    tasks.append((lambda refs: token_of(refs[token]), lambda out: None))
    spare = pl.BlockSpec(memory_space=pl.ANY)
    kept_back = [(i, one) for i, one in enumerate(call.held) if one is not None]
    for array in passed:
        kept_back.append((len(call.shapes), array))
        call.shapes.append(jax.ShapeDtypeStruct(array.shape, array.dtype))
        call.out_specs.append(spare)
    inputs = len(call.operands)
    unused = len(kept_back) + len(after)

    def kernel(side_ref, *refs):
        where = {}
        for i in range(inputs):
            where[("in", i)] = refs[i]
        for i in range(len(call.shapes)):
            where[("out", i)] = refs[inputs + unused + i]
        for work, _ in tasks:
            work(where)

    size = sum(math.prod(shape.shape) for shape in call.shapes)
    out = pl.pallas_call(
        kernel,
        grid_spec=pltpu.PrefetchScalarGridSpec(
            num_scalar_prefetch=1,
            grid=(call.count,),
            in_specs=call.in_specs + [spare] * unused,
            out_specs=call.out_specs,
        ),
        out_shape=call.shapes,
        input_output_aliases={1 + inputs + i: at for i, (at, _) in enumerate(kept_back)},
        compiler_params=params(16 if at_end else 64),
        cost_estimate=pl.CostEstimate(flops=size, bytes_accessed=6 * size, transcendentals=0),
        name="fold",
    )(
        jnp.stack(call.scalars).astype(jnp.int32),
        *call.operands,
        *[array for _, array in kept_back],
        *after,
    )
    for _, finish in tasks:
        finish(lambda write: out[write[1]])
    moving[:] = [one for one in moving if not one.finished]
    return out[token[1]], tuple(out[len(out) - len(passed) :])


def exchange(value, axis, size, bit):
    return lax.ppermute(value, axis, [(i, i ^ bit) for i in range(size)])


def bits_of(size):
    return [1 << i for i in range(size.bit_length() - 1)]


def shards(
    dp_size,
    blk_size,
    embedded,
    species_flag,
    gene_ids,
    species_table,
    norm_gain,
    norm_bias,
    w_qkv,
    w_out,
    w_up,
    w_down,
    out_cotangent,
):
    _, block_len, width = embedded.shape
    half = blk_size // 2
    place = lax.axis_index("blk")
    mine = place // half

    def swap(value):
        return exchange(value, "blk", blk_size, half)

    def own_and_other(pair):
        return tuple(
            lax.dynamic_index_in_dim(pair, which, 0, keepdims=False)
            for which in (mine, 1 - mine)
        )

    def collect(pair):
        own, other = own_and_other(pair)
        return own, swap(other)

    def turn(value, by):
        pairs = []
        for b in range(blk_size):
            base, j = b // half * half, b % half
            pairs.append((b, base + (j - by) % half))
        return lax.ppermute(value, "blk", pairs)

    def gather_parts(value):
        return [value] + [turn(value, by) for by in range(1, half)]

    ids = collect(gene_ids)
    species, _ = own_and_other(species_flag)
    picked = jnp.where(species == 0, species_table[0], species_table[1])
    state = Tokens(collect(embedded), picked[None, :])
    cotangent = Tokens(collect(out_cotangent))

    kept = []
    for layer in range(LAYERS):
        norm = (norm_gain, norm_bias, w_qkv)
        if layer == 0:
            own, away = (Tokens([array], state.shift) for array in state.arrays)
            *some, token = qkv_forward(layer, own, *norm, (), state.rows)
            masked = [jnp.where(part != 0, 0.0, MASKED) + token[0, 0] for part in ids]
            dead = jnp.concatenate(masked).astype(BF16)
            dead_parts = [
                jnp.broadcast_to(part[:, None], (part.shape[0], PAIR))
                for part in gather_parts(dead)
            ]
            h1, q, kv, _ = qkv_forward(layer, away, *norm, (dead,), state.rows, some)
        else:
            h1, q, kv, _ = qkv_forward(layer, state, *norm, ())
        kv_parts = gather_parts(kv)
        att, inverse, p = attend(q, kv_parts, dead_parts)
        last_one = layer == LAYERS - 1
        mid, h2, att_turned, active, slope, *after = feed_forward(
            layer, last_one, att, state, w_out, norm_gain, norm_bias, w_up, w_down
        )
        kept.append(
            (state, h1, q, kv_parts, att, inverse, p, mid, h2, att_turned, active, slope)
        )
        state = Tokens(after)
    came = swap(after[1])
    hidden_out, placed = place_cells(mine[None], after[0], came)

    sizes = {"blk": blk_size, "dp": dp_size}
    places = {"blk": place, "dp": lax.axis_index("dp")}
    core = place % 2
    over_blk = [("blk", bit) for bit in bits_of(blk_size)[1:]]
    over_dp = [("dp", bit) for bit in bits_of(dp_size)]
    core = core[None]

    def column_sums(pair, orders, layer, results, waits):
        gone, own = (value.reshape((half * dp_size,) + value.shape[-2:]) for value in pair)
        came = exchange(gone, "blk", blk_size, 1)
        scatter = waits if layer > 0 else 0
        if own.shape[1] % (16 * len(orders)):
            orders = orders[:1]
        return [
            Sum(came, own, order, sizes, places, layer, results, scatter, (i, len(orders)))
            for i, order in enumerate(orders)
        ]

    up_width = w_up.shape[2] // blk_size
    of_up_out = Results([("up", up_width), ("out", width // blk_size)])
    of_down = Results([("down", w_down.shape[1] // dp_size)])
    of_qkv = Results([("qkv", 3 * width // blk_size)])
    groups = 2
    grad = cotangent
    moving = []
    last = ()
    small = jnp.zeros((16, width), F32)
    species = species[None]
    for layer in reversed(range(LAYERS)):
        x, h1, q, kv_parts, att, inverse, p, mid, h2, att_turned, active, slope = kept[layer]
        up_gone, up_kept, down_gone, down_kept, dmid, datt, small = feed_backward(
            layer,
            grad,
            slope,
            active,
            mid,
            h2,
            att_turned,
            norm_gain,
            w_down,
            w_up,
            w_out,
            small,
            core,
            blk_size,
            dp_size,
            last,
        )
        last = (datt,)
        if moving:
            added, _ = fold(moving, last)
            last = (added,)
        moving += column_sums((up_gone, up_kept), [over_blk + over_dp], layer, of_up_out, 3)
        moving += column_sums((down_gone, down_kept), [over_dp + over_blk], layer, of_down, 3)
        arrived = (came,)
        dq, dkv = [], []
        for group in range(groups):
            one_dq, one_dkv = attend_back(
                group, groups, q, inverse, att, datt, p, kv_parts, last
            )
            others = tuple(one_dkv[1:])
            if group == groups - 1:
                added, others = fold(moving, (one_dq,) + arrived, others)
            else:
                added, _ = fold(moving, (one_dq,) + arrived)
            arrived = tuple(turn(value, half - 1 - by) for by, value in enumerate(others))
            last = (added,)
            dq.append(one_dq)
            dkv.append((one_dkv[0],) + arrived)
        if layer > 0:
            orders = [over_dp + over_blk]
        else:
            near, far = over_dp[:1], over_dp[1:]
            orders = [near + over_blk + far, far[:1] + near + over_blk + far[1:]]
        tiles = 2 * block_len // min(256, block_len)
        ends = tiles if layer > 0 else tiles // 2
        moved = x if layer > 0 else Tokens([x.arrays[1]], x.shift)
        gone, own, one_grad, small = qkv_gradients(
            layer,
            ends,
            F32 if layer > 0 else BF16,
            dq,
            dkv,
            moved,
            norm_gain,
            w_qkv,
            h1,
            dmid,
            small,
            species,
            core,
            blk_size,
            dp_size,
            last,
        )
        if layer == 0:
            added, (one_grad, gone) = fold(moving, (own,), (one_grad, gone))
            last = (added,)
        moving += column_sums((gone, own), orders, layer, of_qkv, 0)
        if layer > 0:
            last = (one_grad,)
            grad = Tokens([one_grad])
        else:
            came = swap(one_grad)
            own_x = Tokens([x.arrays[0]], x.shift)
            own_grad, small = qkv_backward(
                layer, 0, F32, dq, dkv, own_x, norm_gain, w_qkv, dmid, small, species, last
            )
            later = [one for one in moving if one.layer > 0 and one.results is of_qkv]
            moving = [one for one in moving if one not in later]
            added, (small,) = fold(moving, (own_grad,), (small,))
            moving += later
            last = (added,)
    small = SmallSum(small, sizes)
    moving.append(small)
    embed_grad, embed_placed = place_cells(mine[None], own_grad, came)
    last += (placed, embed_placed)
    while moving:
        added, _ = fold(moving, last, (), True)
        last = (added,)

    gain_grad, bias_grad, species_grad = small.value
    return (
        hidden_out,
        embed_grad,
        species_grad,
        gain_grad,
        bias_grad,
        of_qkv.held["qkv"],
        of_up_out.held["out"],
        of_up_out.held["up"],
        of_down.held["down"].transpose(0, 2, 1),
    )


def solution(mesh):
    placed = (
        P("dp", "blk", None),
        P("dp"),
        P("dp", "blk"),
        P(),
        P(),
        P(),
        P(),
        P(),
        P(),
        P(),
        P("dp", "blk", None),
    )
    return jax.shard_map(
        functools.partial(shards, mesh.shape["dp"], mesh.shape["blk"]),
        mesh=mesh,
        in_specs=placed,
        out_specs=(
            P("dp", "blk", None),
            P("dp", "blk", None),
            P(),
            P(),
            P(),
            P(None, "dp", "blk"),
            P(None, "dp", "blk"),
            P(None, "dp", "blk"),
            P(None, "dp", "blk"),
        ),
        check_vma=False,
    )
```
